32 devices in a mesh: dp: 4 (over x, core), ctx: 8 (over z, y).
Axes of the slice: x: 2, y: 2, z: 4, core: 2. Of those that a mesh axis runs over, the one named last changes fastest.
Arguments:
- queries: bfloat16 [4096, 4096], P(('dp', 'ctx')), may hold values from -10 to 10
- keys: bfloat16 [4096, 4096], P(('dp', 'ctx')), may hold values from -10 to 10
- values: bfloat16 [4096, 4096], P(('dp', 'ctx')), may hold values from -6 to 6
- residual_in: bfloat16 [4096, 7168], P(('dp', 'ctx')), may hold values from -40 to 40
- out_weight: bfloat16 [4096, 7168], P('ctx', 'dp'), may hold values from -1.25 to 1.25
- norm_gain: float32 [7168], replicated, may hold values from 0.5 to 1.5
- norm_bias: float32 [7168], replicated, may hold values from -3 to 3
Outputs:
- layer_out: bfloat16 [4096, 7168], P(('dp', 'ctx'))
The draws below stay inside these ranges and needn't reach their ends.
All inputs are finite; a program needn't handle non-finite values.
Results may differ from the reference program's by a relative error of at most 0.0085.
Values may be sent and summed in bfloat16 or wider, within the bound.
A program may use at most 128 MiB of HBM per device.

```python
import math
import jax
import jax.numpy as jnp
from jax import lax

D = 7168
HEADS = 32
HD = 128
SEQ = 1024
TOKENS = 4096
GROUP_HEADS = 4
N_DP = 4
N_CTX = 8


def base_field(key, shape):
    return jnp.clip(jax.random.normal(key, shape, jnp.float32), -4.0, 4.0)


def draw_queries(key, part):
    field = base_field(jax.random.fold_in(key, 1), (TOKENS, HEADS * HD))
    return field.astype(jnp.bfloat16)


def draw_keys(key, part):
    field = base_field(jax.random.fold_in(key, 2), (TOKENS, HEADS * HD))
    return field.astype(jnp.bfloat16)


def draw_residual_in(key, part):
    field = base_field(jax.random.fold_in(key, 3), (TOKENS, D))
    lower, upper = (0.3, 3.0)
    row_scale = jnp.exp(jax.random.uniform(jax.random.fold_in(key, 4), (TOKENS, 1), jnp.float32, math.log(lower), math.log(upper)))
    col_scale = jnp.exp(jax.random.uniform(jax.random.fold_in(key, 5), (1, D), jnp.float32, math.log(lower), math.log(upper)))
    return (field * row_scale * col_scale).astype(jnp.bfloat16)


def levels(stream_key, shape, shards, smallest, top_value):
    level = 1.0
    for axis_at, blocks in shards:
        heights = jax.random.uniform(jax.random.fold_in(jax.random.fold_in(stream_key, 6), axis_at), (blocks,), jnp.float32, smallest / len(shards), top_value / len(shards))
        level = level * jnp.repeat(jnp.exp(heights), shape[axis_at] // blocks).reshape((-1,) + (1,) * (len(shape) - 1 - axis_at))
    return level


def bell_draw(key, dims, deviation, reach, cuts=(), held_as=jnp.bfloat16):
    result = deviation * jax.random.normal(key, dims, jnp.float32)
    if cuts:
        result = result * levels(key, dims, cuts, -0.22, 0.18)
    return jnp.clip(result, -reach, reach).astype(held_as)


def setup_inputs(seed: int = 0) -> dict:
    arg_keys = jax.random.split(jax.random.key(seed), 8)
    return {
        "queries": draw_queries(jax.random.fold_in(arg_keys[7], 71), 0),
        "keys": draw_keys(jax.random.fold_in(arg_keys[7], 71), 0),
        "values": bell_draw(arg_keys[2], (TOKENS, HEADS * HD), 1.0, 6.0, ((0, 32),)),
        "residual_in": draw_residual_in(jax.random.fold_in(arg_keys[7], 71), 0),
        "out_weight": bell_draw(arg_keys[4], (HEADS * HD, D), 0.08, 1.25, ((0, 8), (1, 4))),
        "norm_gain": jnp.clip(jax.random.uniform(arg_keys[5], (D,), jnp.float32, 0.5, 1.5), 0.5, 1.5),
        "norm_bias": bell_draw(arg_keys[6], (D,), 0.5, 3.0, (), jnp.float32),
    }


deepnorm_alpha = 96.0 ** 0.25
norm_eps = 1e-05

def attend(queries, keys, values):
    scale = 1.0 / math.sqrt(HD)
    scores = jnp.einsum('qhd,khd->hqk', queries.astype(jnp.float32), keys.astype(jnp.float32)) * scale
    position = jnp.arange(SEQ)
    causal = position[:, None] >= position[None, :]
    scores = jnp.where(causal[None], scores, -1e+30)
    highest = lax.optimization_barrier(jnp.max(scores, axis=-1, keepdims=True))
    expo = jnp.exp(scores - highest)
    probs = (expo / lax.optimization_barrier(jnp.sum(expo, axis=-1, keepdims=True))).astype(jnp.bfloat16)
    heads_out = jnp.einsum('hqk,khd->qhd', probs.astype(jnp.float32), values.astype(jnp.float32))
    return heads_out.astype(jnp.bfloat16).reshape(SEQ, HEADS * HD)

def reference(queries, keys, values, residual_in, out_weight, norm_gain, norm_bias):
    weight = out_weight.reshape(N_CTX, GROUP_HEADS * HD, D).astype(jnp.float32)

    def one_sequence(inputs):
        seq_q, seq_k, seq_v, seq_x = inputs
        heads_out = attend(seq_q.reshape(SEQ, HEADS, HD), seq_k.reshape(SEQ, HEADS, HD), seq_v.reshape(SEQ, HEADS, HD))
        grouped = heads_out.reshape(SEQ, N_CTX, GROUP_HEADS * HD).astype(jnp.float32)
        group_part = jnp.einsum('sgw,gwd->gsd', grouped, weight)
        group_part = lax.optimization_barrier(group_part.astype(jnp.bfloat16)).astype(jnp.float32)
        attn_out = lax.optimization_barrier(lax.optimization_barrier(jnp.sum(group_part, axis=0)).astype(jnp.bfloat16)).astype(jnp.float32)
        mixed = deepnorm_alpha * seq_x.astype(jnp.float32) + attn_out
        mean = lax.optimization_barrier(jnp.mean(mixed, axis=-1, keepdims=True))
        centered = mixed - mean
        var = lax.optimization_barrier(jnp.mean(centered * centered, axis=-1, keepdims=True))
        normed = centered * lax.rsqrt(var + norm_eps) * norm_gain + norm_bias
        return normed.astype(jnp.bfloat16)
    stacked = (queries.reshape(N_DP, SEQ, HEADS * HD), keys.reshape(N_DP, SEQ, HEADS * HD), values.reshape(N_DP, SEQ, HEADS * HD), residual_in.reshape(N_DP, SEQ, D))
    layer_out = lax.map(one_sequence, stacked)
    return layer_out.reshape(TOKENS, D)
```

```python
import math

import jax
import jax.numpy as jnp
from jax import lax
from jax.experimental import pallas as pl
from jax.experimental.pallas import tpu as pltpu
from jax.sharding import PartitionSpec as P

HEADS = 32


deepnorm_alpha = 96.0**0.25
norm_eps = 1e-05


def block_rows(length):
    block = min(512, length)
    while length % block != 0:
        block = block + 1
    return block


def attend(all_queries, all_keys, all_values, local_heads):
    length = all_queries.shape[0]
    width = all_queries.shape[1]
    head_dim = width // local_heads
    block = block_rows(length)
    blocks = length // block
    scale = 1.0 / math.sqrt(head_dim)
    query_blocks = all_queries.reshape(blocks, block, local_heads, head_dim)
    key_heads = all_keys.reshape(length, local_heads, head_dim)
    value_heads = all_values.reshape(length, local_heads, head_dim)
    key_position = jnp.arange(length)

    def one_block(inputs):
        number, query_part = inputs
        scores = (
            jnp.einsum("qhd,khd->hqk", query_part, key_heads, preferred_element_type=jnp.float32)
            * scale
        )
        query_position = number * block + jnp.arange(block)
        causal = query_position[:, None] >= key_position[None, :]
        scores = jnp.where(causal[None], scores, -1e30)
        highest = jnp.max(scores, axis=-1, keepdims=True)
        expo = jnp.exp(scores - highest)
        probs = (expo / jnp.sum(expo, axis=-1, keepdims=True)).astype(jnp.bfloat16)
        result = jnp.einsum("hqk,khd->qhd", probs, value_heads, preferred_element_type=jnp.float32)
        return result.astype(jnp.bfloat16).reshape(block, width)

    outputs = lax.map(one_block, (jnp.arange(blocks), query_blocks))
    return outputs.reshape(length, width)


def local_general(queries, keys, values, residual_in, out_weight, norm_gain, norm_bias):
    head_q, head_k, head_v = (
        lax.all_to_all(queries, "ctx", split_axis=1, concat_axis=0, tiled=True),
        lax.all_to_all(keys, "ctx", split_axis=1, concat_axis=0, tiled=True),
        lax.all_to_all(values, "ctx", split_axis=1, concat_axis=0, tiled=True),
    )
    groups = lax.axis_size("ctx")
    attn_heads = attend(head_q, head_k, head_v, HEADS // groups)
    group_rows = lax.all_gather(out_weight, "dp", axis=1, tiled=True)
    summed = lax.psum_scatter(
        jnp.dot(attn_heads, group_rows, preferred_element_type=jnp.float32).astype(jnp.bfloat16),
        "ctx",
        scatter_dimension=0,
        tiled=True,
    )
    attn_float = lax.optimization_barrier(summed).astype(jnp.float32)
    mixed = deepnorm_alpha * residual_in.astype(jnp.float32) + attn_float
    mean = jnp.mean(mixed, axis=-1, keepdims=True)
    centered = mixed - mean
    var = jnp.mean(centered * centered, axis=-1, keepdims=True)
    normed = centered * lax.rsqrt(var + norm_eps) * norm_gain + norm_bias
    return normed.astype(jnp.bfloat16)


MESH = pl.DeviceIdType.MESH
CHUNKS = 8


def fused_kernel(
    q_ref, k_ref, v_ref, w_ref, res_ref, gain_ref, bias_ref, out_ref,
    qh, kh, vh, wf, op, ostage, upr, dnr, ups, dns, own, pbuf,
    s_send, s_recv, s_local, w_send, w_recv, w_local, o_send, o_recv,
    up_send, up_recv, dn_send, dn_recv,
):
    rows = q_ref.shape[0]
    hd = qh.shape[2]
    heads = qh.shape[0]
    group = heads * hd
    half = w_ref.shape[0] // 2
    chunk = own.shape[2]
    dp = lax.axis_index("dp")
    ctx = lax.axis_index("ctx")
    xi, core = dp // 2, dp % 2
    zi, yi = ctx // 2, ctx % 2
    sib = (xi * 2 + (1 - core), ctx)
    xnb = ((1 - xi) * 2 + core, ctx)
    ynb = (dp, zi * 2 + (1 - yi))

    barrier = pltpu.get_barrier_semaphore()
    for d in range(1, 8):
        pl.semaphore_signal(barrier, inc=1, device_id=(dp, (ctx + d) % 8), device_id_type=MESH)
    for peer in (sib, xnb):
        pl.semaphore_signal(barrier, inc=1, device_id=peer, device_id_type=MESH)
    pl.semaphore_wait(barrier, 9)

    sources = (q_ref, k_ref, v_ref)
    landing = (qh, kh, vh)

    def cols_of(target, h):
        return pl.ds(pl.multiple_of(target * group + h * hd, hd), hd)

    def rows_of(block):
        return pl.ds(pl.multiple_of(block * rows, rows), rows)

    def qkv_copy(a, h, target):
        return pltpu.make_async_remote_copy(
            src_ref=sources[a].at[:, cols_of(target, h)],
            dst_ref=landing[a].at[h, rows_of(ctx), :],
            send_sem=s_send.at[a, h, target],
            recv_sem=s_recv.at[a, h, ctx],
            device_id=(dp, target),
            device_id_type=MESH,
        )

    def qkv_arrival(a, h, source):
        place = landing[a].at[h, rows_of(source), :]
        return pltpu.make_async_remote_copy(
            src_ref=place, dst_ref=place,
            send_sem=s_send.at[a, h, source], recv_sem=s_recv.at[a, h, source],
            device_id=(dp, source), device_id_type=MESH,
        )

    def qkv_local(a, h):
        return pltpu.make_async_copy(
            sources[a].at[:, cols_of(ctx, h)], landing[a].at[h, rows_of(ctx), :], s_local.at[a, h]
        )

    def w_slot(y, d, part):
        return wf.at[y, d, pl.ds(part * half, half), :]

    def w_copy(slot_y, slot_d, part, peer, number, first=False):
        place = w_slot(slot_y, slot_d, part)
        return pltpu.make_async_remote_copy(
            src_ref=w_ref.at[pl.ds(part * half, half), :] if first else place,
            dst_ref=place,
            send_sem=w_send.at[number, part],
            recv_sem=w_recv.at[slot_y, slot_d, part],
            device_id=peer,
            device_id_type=MESH,
        )

    def own_w(number, part):
        return w_copy(yi, dp, part, (xnb, ynb, sib)[number], number, True)

    xdp = xnb[0]
    forwards = {
        3: (yi, xdp, sib),
        4: (1 - yi, dp, sib),
        5: (1 - yi, dp, xnb),
        6: (1 - yi, xdp, sib),
    }

    def forward(number, part):
        slot_y, slot_d, peer = forwards[number]
        return w_copy(slot_y, slot_d, part, peer, number)

    keep_w = pltpu.make_async_copy(w_ref, wf.at[yi, dp], w_local.at[0])

    for h in range(heads):
        for d in (4, 3, 5, 2, 6, 1, 7):
            for a in range(3):
                qkv_copy(a, h, (ctx + d) % 8).start()
        for a in range(3):
            qkv_local(a, h).start()
        if h < 3:
            for part in range(2):
                own_w(h, part).start()
    keep_w.start()

    factor = math.log2(math.e) / math.sqrt(hd)
    block = 2 * rows

    def o_copy(h):
        return pltpu.make_async_remote_copy(
            src_ref=ostage.at[h],
            dst_ref=op.at[yi, h],
            send_sem=o_send.at[h],
            recv_sem=o_recv.at[h],
            device_id=ynb,
            device_id_type=MESH,
        )

    def one_head(h, carry):
        def arrived(d, inner):
            for a in range(3):
                qkv_arrival(a, h, (ctx + d) % 8).wait_recv()
            return inner

        lax.fori_loop(1, 8, arrived, 0)
        for a in range(3):
            qkv_local(a, h).wait()
        for t in range(4):
            length = block * (t + 1)
            scores = lax.dot_general(
                qh[h, t * block : length, :], kh[h, :length, :],
                (((1,), (1,)), ((), ())), preferred_element_type=jnp.float32,
            )
            at_row = lax.broadcasted_iota(jnp.int32, (block, length), 0) + t * block
            at_col = lax.broadcasted_iota(jnp.int32, (block, length), 1)
            scores = jnp.where(at_row >= at_col, scores, -1e30)
            highest = jnp.max(scores, axis=-1, keepdims=True)
            expo = jnp.exp2((scores - highest) * factor)
            total = jnp.sum(expo, axis=-1, keepdims=True)
            result = jnp.dot(
                expo.astype(jnp.bfloat16), vh[h, :length, :], preferred_element_type=jnp.float32
            ) / total
            low, high = result[:rows], result[rows:]
            mine = jnp.where(yi == 0, low, high)
            theirs = jnp.where(yi == 0, high, low)
            op[yi, h, t * rows : (t + 1) * rows, :] = mine.astype(jnp.bfloat16)
            ostage[h, t * rows : (t + 1) * rows, :] = theirs.astype(jnp.bfloat16)
        o_copy(h).start()

        @pl.when(h == 1)
        def _():
            for part in range(2):
                w_copy(yi, xdp, part, xnb, 0).wait_recv()
                forward(3, part).start()

        return carry

    lax.fori_loop(0, heads, one_head, 0)

    for part in range(2):
        w_copy(1 - yi, dp, part, ynb, 1).wait_recv()
        forward(5, part).start()
        forward(4, part).start()
    for h in range(heads):
        place = op.at[1 - yi, h]
        pltpu.make_async_remote_copy(
            src_ref=place, dst_ref=place, send_sem=o_send.at[h], recv_sem=o_recv.at[h],
            device_id=ynb, device_id_type=MESH,
        ).wait_recv()
    keep_w.wait()

    def chain_copy(up, t, c):
        slot = t - 1 if up else t
        to = jnp.minimum(zi + 1, 3) if up else jnp.maximum(zi - 1, 0)
        return pltpu.make_async_remote_copy(
            src_ref=(ups if up else dns).at[slot, c],
            dst_ref=(upr if up else dnr).at[slot, c],
            send_sem=(up_send if up else dn_send).at[slot, c],
            recv_sem=(up_recv if up else dn_recv).at[slot, c],
            device_id=(dp, to * 2 + yi),
            device_id_type=MESH,
        )

    def relay(up, t, c, allowed):
        slot = t - 1 if up else t
        here, there = (ups, upr) if up else (dns, dnr)
        sends = jnp.logical_and(allowed, zi < t if up else zi > t)
        origin = zi == 0 if up else zi == 3

        @pl.when(jnp.logical_and(sends, origin))
        def _():
            here[slot, c] = pbuf[t].astype(jnp.bfloat16)
            chain_copy(up, t, c).start()

        @pl.when(jnp.logical_and(sends, jnp.logical_not(origin)))
        def _():
            chain_copy(up, t, c).wait_recv()
            here[slot, c] = (pbuf[t] + there[slot, c].astype(jnp.float32)).astype(jnp.bfloat16)
            chain_copy(up, t, c).start()

    def one_chunk(n, carry):
        i, j = n // 2, n % 2
        d = ((xi + i // 2) % 2) * 2 + (core + i % 2) % 2
        c = d * 2 + j

        @pl.when(n % 4 == 2)
        def _():
            for y in range(2):
                for part in range(2):
                    w_copy(y, d, part, sib, 2).wait_recv()

        @pl.when(n == 3)
        def _():
            for part in range(2):
                w_copy(1 - yi, xdp, part, xnb, 5).wait_recv()
                forward(6, part).start()

        cols = pl.ds(pl.multiple_of(j * chunk, 128), chunk)
        lhs = jnp.concatenate([op[y, h] for y in range(2) for h in range(heads)], axis=1)
        rhs = wf[:, d, :, cols].reshape(2 * group, chunk)
        pbuf[...] = jnp.dot(lhs, rhs, preferred_element_type=jnp.float32).reshape(pbuf.shape)
        lower = zi < 2
        upper = zi >= 2
        relay(True, 3, c, lower)
        relay(False, 0, c, upper)
        relay(True, 3, c, upper)
        relay(False, 0, c, lower)
        always = zi >= 0
        relay(True, 2, c, always)
        relay(False, 1, c, always)
        relay(True, 1, c, always)
        relay(False, 2, c, always)
        own[c] = pbuf[zi]
        return carry

    lax.fori_loop(0, CHUNKS, one_chunk, 0)

    width = chunk * CHUNKS

    def arrive(n, carry):
        i, j = n // 2, n % 2
        d = ((xi + i // 2) % 2) * 2 + (core + i % 2) % 2
        c = d * 2 + j

        @pl.when(zi > 0)
        def _():
            place = upr.at[zi - 1, c]
            pltpu.make_async_remote_copy(
                src_ref=place, dst_ref=place, send_sem=up_send.at[zi - 1, c],
                recv_sem=up_recv.at[zi - 1, c], device_id=ynb, device_id_type=MESH,
            ).wait_recv()
            own[c] += upr[zi - 1, c].astype(jnp.float32)

        @pl.when(zi < 3)
        def _():
            place = dnr.at[zi, c]
            pltpu.make_async_remote_copy(
                src_ref=place, dst_ref=place, send_sem=dn_send.at[zi, c],
                recv_sem=dn_recv.at[zi, c], device_id=ynb, device_id_type=MESH,
            ).wait_recv()
            own[c] += dnr[zi, c].astype(jnp.float32)

        return carry

    lax.fori_loop(0, CHUNKS, arrive, 0)

    total = jnp.zeros((rows, 1), jnp.float32)
    for c in range(CHUNKS):
        res = res_ref[:, c * chunk : (c + 1) * chunk].astype(jnp.float32)
        mixed = deepnorm_alpha * res + own[c].astype(jnp.bfloat16).astype(jnp.float32)
        own[c] = mixed
        total += jnp.sum(mixed, axis=-1, keepdims=True)
    mean = total / width
    squares = jnp.zeros((rows, 1), jnp.float32)
    for c in range(CHUNKS):
        centered = own[c] - mean
        squares += jnp.sum(centered * centered, axis=-1, keepdims=True)
    inverse = lax.rsqrt(squares / width + norm_eps)
    for c in range(CHUNKS):
        normed = (own[c] - mean) * inverse * gain_ref[c] + bias_ref[c]
        out_ref[:, c * chunk : (c + 1) * chunk] = normed.astype(out_ref.dtype)

    def sent_qkv(h, carry):
        def sent(d, inner):
            for a in range(3):
                qkv_copy(a, h, (ctx + d) % 8).wait_send()
            return inner

        lax.fori_loop(1, 8, sent, 0)
        o_copy(h).wait_send()
        return carry

    lax.fori_loop(0, heads, sent_qkv, 0)
    for part in range(2):
        for number in range(3):
            own_w(number, part).wait_send()
        for number in forwards:
            forward(number, part).wait_send()

    def sent_chain(c, carry):
        for t in range(1, 4):
            @pl.when(zi < t)
            def _():
                chain_copy(True, t, c).wait_send()
        for t in range(3):
            @pl.when(zi > t)
            def _():
                chain_copy(False, t, c).wait_send()
        return carry

    lax.fori_loop(0, CHUNKS, sent_chain, 0)


def local_fused(queries, keys, values, residual_in, out_weight, norm_gain, norm_bias):
    rows, width = residual_in.shape
    group, columns = out_weight.shape
    hd = queries.shape[1] // HEADS
    heads = group // hd
    length = rows * 8
    chunk = width // CHUNKS
    bf16, f32 = jnp.bfloat16, jnp.float32
    dma = pltpu.SemaphoreType.DMA
    in_vmem = pl.BlockSpec(memory_space=pltpu.VMEM)
    in_any = pl.BlockSpec(memory_space=pl.ANY)
    return pl.pallas_call(
        fused_kernel,
        out_shape=jax.ShapeDtypeStruct((rows, width), bf16),
        in_specs=[in_any] * 4 + [in_vmem] * 3,
        out_specs=in_vmem,
        scratch_shapes=[
            pltpu.VMEM((heads, length, hd), bf16),
            pltpu.VMEM((heads, length, hd), bf16),
            pltpu.VMEM((heads, length, hd), bf16),
            pltpu.VMEM((2, 4, group, columns), bf16),
            pltpu.VMEM((2, heads, length // 2, hd), bf16),
            pltpu.VMEM((heads, length // 2, hd), bf16),
            pltpu.VMEM((3, CHUNKS, rows, chunk), bf16),
            pltpu.VMEM((3, CHUNKS, rows, chunk), bf16),
            pltpu.VMEM((3, CHUNKS, rows, chunk), bf16),
            pltpu.VMEM((3, CHUNKS, rows, chunk), bf16),
            pltpu.VMEM((CHUNKS, rows, chunk), f32),
            pltpu.VMEM((4, rows, chunk), f32),
            dma((3, heads, 8)), dma((3, heads, 8)), dma((3, heads)),
            dma((7, 2)), dma((2, 4, 2)), dma((1,)),
            dma((heads,)), dma((heads,)),
            dma((3, CHUNKS)), dma((3, CHUNKS)), dma((3, CHUNKS)), dma((3, CHUNKS)),
        ],
        compiler_params=pltpu.CompilerParams(
            collective_id=0, has_side_effects=True, vmem_limit_bytes=60 * 1024 * 1024
        ),
    )(
        queries, keys, values, out_weight, residual_in,
        norm_gain.reshape(CHUNKS, 1, chunk), norm_bias.reshape(CHUNKS, 1, chunk),
    )


def solution(mesh):
    in_specs = (
        P(("dp", "ctx"), None),
        P(("dp", "ctx"), None),
        P(("dp", "ctx"), None),
        P(("dp", "ctx"), None),
        P("ctx", "dp"),
        P(),
        P(),
    )
    out_specs = P(("dp", "ctx"), None)
    fused = mesh.shape["dp"] == 4 and mesh.shape["ctx"] == 8
    local = local_fused if fused else local_general
    return jax.shard_map(local, mesh=mesh, in_specs=in_specs, out_specs=out_specs, check_vma=False)
```

```python
import math

import jax
import jax.numpy as jnp
from jax import lax
from jax.experimental import pallas as pl
from jax.experimental.pallas import tpu as pltpu
from jax.sharding import PartitionSpec as P

HEADS = 32


deepnorm_alpha = 96.0**0.25
norm_eps = 1e-05


def block_rows(length):
    block = min(512, length)
    while length % block != 0:
        block = block + 1
    return block


def attend(all_queries, all_keys, all_values, local_heads):
    length = all_queries.shape[0]
    width = all_queries.shape[1]
    head_dim = width // local_heads
    block = block_rows(length)
    blocks = length // block
    scale = 1.0 / math.sqrt(head_dim)
    query_blocks = all_queries.reshape(blocks, block, local_heads, head_dim)
    key_heads = all_keys.reshape(length, local_heads, head_dim)
    value_heads = all_values.reshape(length, local_heads, head_dim)
    key_position = jnp.arange(length)

    def one_block(inputs):
        number, query_part = inputs
        scores = (
            jnp.einsum("qhd,khd->hqk", query_part, key_heads, preferred_element_type=jnp.float32)
            * scale
        )
        query_position = number * block + jnp.arange(block)
        causal = query_position[:, None] >= key_position[None, :]
        scores = jnp.where(causal[None], scores, -1e30)
        highest = jnp.max(scores, axis=-1, keepdims=True)
        expo = jnp.exp(scores - highest)
        probs = (expo / jnp.sum(expo, axis=-1, keepdims=True)).astype(jnp.bfloat16)
        result = jnp.einsum("hqk,khd->qhd", probs, value_heads, preferred_element_type=jnp.float32)
        return result.astype(jnp.bfloat16).reshape(block, width)

    outputs = lax.map(one_block, (jnp.arange(blocks), query_blocks))
    return outputs.reshape(length, width)


def local_general(queries, keys, values, residual_in, out_weight, norm_gain, norm_bias):
    head_q, head_k, head_v = (
        lax.all_to_all(queries, "ctx", split_axis=1, concat_axis=0, tiled=True),
        lax.all_to_all(keys, "ctx", split_axis=1, concat_axis=0, tiled=True),
        lax.all_to_all(values, "ctx", split_axis=1, concat_axis=0, tiled=True),
    )
    groups = lax.axis_size("ctx")
    attn_heads = attend(head_q, head_k, head_v, HEADS // groups)
    group_rows = lax.all_gather(out_weight, "dp", axis=1, tiled=True)
    summed = lax.psum_scatter(
        jnp.dot(attn_heads, group_rows, preferred_element_type=jnp.float32).astype(jnp.bfloat16),
        "ctx",
        scatter_dimension=0,
        tiled=True,
    )
    attn_float = lax.optimization_barrier(summed).astype(jnp.float32)
    mixed = deepnorm_alpha * residual_in.astype(jnp.float32) + attn_float
    mean = jnp.mean(mixed, axis=-1, keepdims=True)
    centered = mixed - mean
    var = jnp.mean(centered * centered, axis=-1, keepdims=True)
    normed = centered * lax.rsqrt(var + norm_eps) * norm_gain + norm_bias
    return normed.astype(jnp.bfloat16)


MESH = pl.DeviceIdType.MESH
CHUNKS = 8


def fused_kernel(
    q_ref, k_ref, v_ref, w_ref, res_ref, gain_ref, bias_ref, out_ref,
    qh, kh, vh, wf, wf2, op, op2, ostage, upr, dnr, stage, own, pbuf,
    s_send, s_recv, s_local, w_send, w_recv, w_local, w2_send, w2_recv,
    o_send, o_recv, o2_send, o2_recv,
    up_send, up_recv, dn_send, dn_recv,
):
    rows = q_ref.shape[0]
    hd = qh.shape[2]
    heads = qh.shape[0]
    group = heads * hd
    half = w_ref.shape[0] // 2
    chunk = own.shape[2]
    dp = lax.axis_index("dp")
    ctx = lax.axis_index("ctx")
    xi, core = dp // 2, dp % 2
    zi, yi = ctx // 2, ctx % 2
    sib = (xi * 2 + (1 - core), ctx)
    xnb = ((1 - xi) * 2 + core, ctx)
    ynb = (dp, zi * 2 + (1 - yi))
    is_hub = jnp.logical_and(zi >= 1, zi <= 2)
    is_feeder = jnp.logical_or(zi == 0, zi == 3)
    hub = 1 + zi // 2
    feeder = (zi // 2) * 3

    barrier = pltpu.get_barrier_semaphore()
    for d in range(1, 8):
        pl.semaphore_signal(barrier, inc=1, device_id=(dp, (ctx + d) % 8), device_id_type=MESH)
    for peer in (sib, xnb):
        pl.semaphore_signal(barrier, inc=1, device_id=peer, device_id_type=MESH)
    pl.semaphore_wait(barrier, 9)

    sources = (q_ref, k_ref, v_ref)
    landing = (qh, kh, vh)

    def cols_of(target, h):
        return pl.ds(pl.multiple_of(target * group + h * hd, hd), hd)

    def rows_of(block):
        return pl.ds(pl.multiple_of(block * rows, rows), rows)

    def qkv_copy(a, h, target):
        return pltpu.make_async_remote_copy(
            src_ref=sources[a].at[:, cols_of(target, h)],
            dst_ref=landing[a].at[h, rows_of(ctx), :],
            send_sem=s_send.at[a, h, target],
            recv_sem=s_recv.at[a, h, ctx],
            device_id=(dp, target),
            device_id_type=MESH,
        )

    def qkv_arrival(a, h, source):
        place = landing[a].at[h, rows_of(source), :]
        return pltpu.make_async_remote_copy(
            src_ref=place, dst_ref=place,
            send_sem=s_send.at[a, h, source], recv_sem=s_recv.at[a, h, source],
            device_id=(dp, source), device_id_type=MESH,
        )

    def qkv_local(a, h):
        return pltpu.make_async_copy(
            sources[a].at[:, cols_of(ctx, h)], landing[a].at[h, rows_of(ctx), :], s_local.at[a, h]
        )

    def w_copy(slot_y, slot_d, part, peer, number, first=False):
        place = wf.at[slot_y, slot_d, pl.ds(part * half, half), :]
        return pltpu.make_async_remote_copy(
            src_ref=w_ref.at[pl.ds(part * half, half), :] if first else place,
            dst_ref=place,
            send_sem=w_send.at[number, part],
            recv_sem=w_recv.at[slot_y, slot_d, part],
            device_id=peer,
            device_id_type=MESH,
        )

    def own_w(number, part):
        return w_copy(yi, dp, part, (xnb, ynb, sib)[number], number, True)

    xdp = xnb[0]
    forwards = {
        3: (yi, xdp, sib),
        4: (1 - yi, dp, sib),
        5: (1 - yi, dp, xnb),
        6: (1 - yi, xdp, sib),
    }

    def forward(number, part):
        slot_y, slot_d, peer = forwards[number]
        return w_copy(slot_y, slot_d, part, peer, number)

    def w2_copy(slot_y, slot_d, part, peer, number, first=False):
        place = wf2.at[slot_y, slot_d, pl.ds(part * half, half), :]
        return pltpu.make_async_remote_copy(
            src_ref=w_ref.at[pl.ds(part * half, half), pl.ds(0, chunk)] if first else place,
            dst_ref=place,
            send_sem=w2_send.at[number, part],
            recv_sem=w2_recv.at[slot_y, slot_d, part],
            device_id=peer,
            device_id_type=MESH,
        )

    def feed_w2(part):
        return w2_copy(yi, dp, part, (dp, hub * 2 + yi), 7, True)

    spreads = {0: (yi, dp, xnb), 1: (yi, dp, ynb), 2: (yi, dp, sib)}
    spreads.update(forwards)

    def forward2(number, part):
        slot_y, slot_d, peer = spreads[number]
        return w2_copy(slot_y, slot_d, part, peer, number)

    keep_w = pltpu.make_async_copy(w_ref, wf.at[yi, dp], w_local.at[0])

    for h in range(heads):
        for d in (4, 3, 5, 2, 6, 1, 7):
            for a in range(3):
                qkv_copy(a, h, (ctx + d) % 8).start()
        for a in range(3):
            qkv_local(a, h).start()
        if h < 3:
            for part in range(2):
                own_w(h, part).start()
        if h == 1:
            @pl.when(is_feeder)
            def _():
                for part in range(2):
                    feed_w2(part).start()
    keep_w.start()

    factor = math.log2(math.e) / math.sqrt(hd)
    block = 2 * rows

    def o_copy(h):
        return pltpu.make_async_remote_copy(
            src_ref=ostage.at[h],
            dst_ref=op.at[yi, h],
            send_sem=o_send.at[h],
            recv_sem=o_recv.at[h],
            device_id=ynb,
            device_id_type=MESH,
        )

    def feed_o(h, same):
        to = yi if same else 1 - yi
        return pltpu.make_async_remote_copy(
            src_ref=op.at[yi, h] if same else ostage.at[h],
            dst_ref=op2.at[yi, h],
            send_sem=o2_send.at[0 if same else 1, h],
            recv_sem=o2_recv.at[yi, h],
            device_id=(dp, hub * 2 + to),
            device_id_type=MESH,
        )

    def one_head(h, carry):
        def arrived(d, inner):
            for a in range(3):
                qkv_arrival(a, h, (ctx + d) % 8).wait_recv()
            return inner

        lax.fori_loop(1, 8, arrived, 0)
        for a in range(3):
            qkv_local(a, h).wait()
        for t in range(4):
            length = block * (t + 1)
            scores = lax.dot_general(
                qh[h, t * block : length, :], kh[h, :length, :],
                (((1,), (1,)), ((), ())), preferred_element_type=jnp.float32,
            )
            at_row = lax.broadcasted_iota(jnp.int32, (block, length), 0) + t * block
            at_col = lax.broadcasted_iota(jnp.int32, (block, length), 1)
            scores = jnp.where(at_row >= at_col, scores, -1e30)
            highest = jnp.max(scores, axis=-1, keepdims=True)
            expo = jnp.exp2((scores - highest) * factor)
            total = jnp.sum(expo, axis=-1, keepdims=True)
            result = jnp.dot(
                expo.astype(jnp.bfloat16), vh[h, :length, :], preferred_element_type=jnp.float32
            ) / total
            low, high = result[:rows], result[rows:]
            mine = jnp.where(yi == 0, low, high)
            theirs = jnp.where(yi == 0, high, low)
            op[yi, h, t * rows : (t + 1) * rows, :] = mine.astype(jnp.bfloat16)
            ostage[h, t * rows : (t + 1) * rows, :] = theirs.astype(jnp.bfloat16)
        o_copy(h).start()

        @pl.when(is_feeder)
        def _():
            feed_o(h, True).start()
            feed_o(h, False).start()

        @pl.when(jnp.logical_and(h == 2, is_hub))
        def _():
            for part in range(2):
                w2_copy(yi, dp, part, ynb, 0).wait_recv()
                for number in range(3):
                    forward2(number, part).start()

        @pl.when(h == 1)
        def _():
            for part in range(2):
                w_copy(yi, xdp, part, xnb, 0).wait_recv()
                forward(3, part).start()

        return carry

    lax.fori_loop(0, heads, one_head, 0)

    for part in range(2):
        w_copy(1 - yi, dp, part, ynb, 1).wait_recv()
        forward(5, part).start()
        forward(4, part).start()
    for h in range(heads):
        place = op.at[1 - yi, h]
        pltpu.make_async_remote_copy(
            src_ref=place, dst_ref=place, send_sem=o_send.at[h], recv_sem=o_recv.at[h],
            device_id=ynb, device_id_type=MESH,
        ).wait_recv()
    keep_w.wait()

    def chain_copy(up, t, c):
        slot = t - 1 if up else t
        to = jnp.minimum(zi + 1, 3) if up else jnp.maximum(zi - 1, 0)
        return pltpu.make_async_remote_copy(
            src_ref=stage.at[slot, c],
            dst_ref=(upr if up else dnr).at[slot, c],
            send_sem=(up_send if up else dn_send).at[slot, c],
            recv_sem=(up_recv if up else dn_recv).at[slot, c],
            device_id=(dp, to * 2 + yi),
            device_id_type=MESH,
        )

    def sends_here(up, t, hubs):
        sends = zi < t if up else zi > t
        if hubs:
            sends = jnp.logical_and(sends, zi >= 1 if up else zi <= 2)
        return sends

    def relay(up, t, c, hubs, allowed):
        slot = t - 1 if up else t
        there = upr if up else dnr
        sends = jnp.logical_and(allowed, sends_here(up, t, hubs))
        first = (1 if hubs else 0) if up else (2 if hubs else 3)

        @pl.when(jnp.logical_and(sends, zi == first))
        def _():
            stage[slot, c] = pbuf[t].astype(jnp.bfloat16)
            chain_copy(up, t, c).start()

        @pl.when(jnp.logical_and(sends, zi != first))
        def _():
            chain_copy(up, t, c).wait_recv()
            stage[slot, c] = (pbuf[t] + there[slot, c].astype(jnp.float32)).astype(jnp.bfloat16)
            chain_copy(up, t, c).start()

    def relays(c, hubs):
        lower, upper = zi < 2, zi >= 2
        ups = (3, 2) if hubs else (3, 2, 1)
        downs = (0, 1) if hubs else (0, 1, 2)
        for t in ups:
            relay(True, t, c, hubs, lower)
        for t in downs:
            relay(False, t, c, hubs, upper)
        for t in ups:
            relay(True, t, c, hubs, upper)
        for t in downs:
            relay(False, t, c, hubs, lower)

    def owner(i):
        return ((xi + i // 2) % 2) * 2 + (core + i % 2) % 2

    def wait_chain(up, slot, c):
        place = (upr if up else dnr).at[slot, c]
        pltpu.make_async_remote_copy(
            src_ref=place, dst_ref=place, send_sem=(up_send if up else dn_send).at[slot, c],
            recv_sem=(up_recv if up else dn_recv).at[slot, c], device_id=ynb, device_id_type=MESH,
        ).wait_recv()

    def finish(i, total):
        for j in (1, 0):
            c = owner(i) * 2 + j

            @pl.when(zi > (1 if j == 0 else 0))
            def _():
                wait_chain(True, zi - 1, c)
                own[c] += upr[zi - 1, c].astype(jnp.float32)

            @pl.when(zi < (2 if j == 0 else 3))
            def _():
                wait_chain(False, zi, c)
                own[c] += dnr[zi, c].astype(jnp.float32)

            res = res_ref[:, pl.ds(pl.multiple_of(c * chunk, 128), chunk)].astype(jnp.float32)
            mixed = deepnorm_alpha * res + own[c].astype(jnp.bfloat16).astype(jnp.float32)
            own[c] = mixed
            total = total + jnp.sum(mixed, axis=-1, keepdims=True)
        return total

    def heads_of(ref):
        return jnp.concatenate([ref[y, h] for y in range(2) for h in range(heads)], axis=1)

    def product(lhs, rhs):
        return jnp.dot(
            lhs, rhs.reshape(2 * group, chunk), preferred_element_type=jnp.float32
        ).reshape(pbuf.shape)

    def one_step(i, total):
        d = owner(i)

        @pl.when(i % 2 == 1)
        def _():
            for y in range(2):
                for part in range(2):
                    w_copy(y, d, part, sib, 2).wait_recv()

        c = d * 2 + 1
        pbuf[...] = product(heads_of(op), wf[:, d, :, pl.ds(chunk, chunk)])
        relays(c, False)
        own[c] = pbuf[zi]

        @pl.when(i == 1)
        def _():
            for part in range(2):
                w_copy(1 - yi, xdp, part, xnb, 5).wait_recv()
                forward(6, part).start()

        c0 = d * 2

        @pl.when(is_hub)
        def _():
            @pl.when(i == 0)
            def _():
                for part in range(2):
                    w2_copy(1 - yi, dp, part, ynb, 1).wait_recv()
                    forward2(5, part).start()
                    forward2(4, part).start()
                for part in range(2):
                    w2_copy(yi, xdp, part, xnb, 0).wait_recv()
                    forward2(3, part).start()
                for h in range(heads):
                    for y in range(2):
                        place = op2.at[y, h]
                        pltpu.make_async_remote_copy(
                            src_ref=place, dst_ref=place, send_sem=o2_send.at[0, h],
                            recv_sem=o2_recv.at[y, h], device_id=ynb, device_id_type=MESH,
                        ).wait_recv()

            @pl.when(i % 2 == 1)
            def _():
                for y in range(2):
                    for part in range(2):
                        w2_copy(y, d, part, sib, 2).wait_recv()

            pbuf[...] = product(heads_of(op), wf[:, d, :, pl.ds(0, chunk)])
            pbuf[...] += product(heads_of(op2), wf2[:, d])
            relays(c0, True)
            own[c0] = pbuf[zi]

            @pl.when(i == 1)
            def _():
                for part in range(2):
                    w2_copy(1 - yi, xdp, part, xnb, 5).wait_recv()
                    forward2(6, part).start()

        @pl.when(is_feeder)
        def _():
            own[c0] = jnp.zeros(own.shape[1:], jnp.float32)

        return lax.cond(i > 0, lambda: finish(i - 1, total), lambda: total)

    total = lax.fori_loop(0, 4, one_step, jnp.zeros((rows, 1), jnp.float32))
    total = finish(3, total)

    width = chunk * CHUNKS
    mean = total / width
    squares = jnp.zeros((rows, 1), jnp.float32)
    for c in range(CHUNKS):
        centered = own[c] - mean
        squares += jnp.sum(centered * centered, axis=-1, keepdims=True)
    inverse = lax.rsqrt(squares / width + norm_eps)
    for c in range(CHUNKS):
        normed = (own[c] - mean) * inverse * gain_ref[c] + bias_ref[c]
        out_ref[:, c * chunk : (c + 1) * chunk] = normed.astype(out_ref.dtype)

    def sent_qkv(h, carry):
        def sent(d, inner):
            for a in range(3):
                qkv_copy(a, h, (ctx + d) % 8).wait_send()
            return inner

        lax.fori_loop(1, 8, sent, 0)
        o_copy(h).wait_send()

        @pl.when(is_feeder)
        def _():
            feed_o(h, True).wait_send()
            feed_o(h, False).wait_send()

        return carry

    lax.fori_loop(0, heads, sent_qkv, 0)
    for part in range(2):
        for number in range(3):
            own_w(number, part).wait_send()
        for number in forwards:
            forward(number, part).wait_send()

    @pl.when(is_feeder)
    def _():
        for part in range(2):
            feed_w2(part).wait_send()

    @pl.when(is_hub)
    def _():
        for part in range(2):
            for number in spreads:
                forward2(number, part).wait_send()

    def sent_chain(d, carry):
        for j in range(2):
            for up, targets in ((True, (3, 2, 1)), (False, (0, 1, 2))):
                for t in targets:
                    @pl.when(sends_here(up, t, j == 0))
                    def _():
                        chain_copy(up, t, d * 2 + j).wait_send()
        return carry

    lax.fori_loop(0, CHUNKS // 2, sent_chain, 0)


def local_fused(queries, keys, values, residual_in, out_weight, norm_gain, norm_bias):
    rows, width = residual_in.shape
    group, columns = out_weight.shape
    hd = queries.shape[1] // HEADS
    heads = group // hd
    length = rows * 8
    chunk = width // CHUNKS
    bf16, f32 = jnp.bfloat16, jnp.float32
    dma = pltpu.SemaphoreType.DMA
    in_vmem = pl.BlockSpec(memory_space=pltpu.VMEM)
    in_any = pl.BlockSpec(memory_space=pl.ANY)
    return pl.pallas_call(
        fused_kernel,
        out_shape=jax.ShapeDtypeStruct((rows, width), bf16),
        in_specs=[in_any] * 4 + [in_vmem] * 3,
        out_specs=in_vmem,
        scratch_shapes=[
            pltpu.VMEM((heads, length, hd), bf16),
            pltpu.VMEM((heads, length, hd), bf16),
            pltpu.VMEM((heads, length, hd), bf16),
            pltpu.VMEM((2, 4, group, columns), bf16),
            pltpu.VMEM((2, 4, group, chunk), bf16),
            pltpu.VMEM((2, heads, length // 2, hd), bf16),
            pltpu.VMEM((2, heads, length // 2, hd), bf16),
            pltpu.VMEM((heads, length // 2, hd), bf16),
            pltpu.VMEM((3, CHUNKS, rows, chunk), bf16),
            pltpu.VMEM((3, CHUNKS, rows, chunk), bf16),
            pltpu.VMEM((3, CHUNKS, rows, chunk), bf16),
            pltpu.VMEM((CHUNKS, rows, chunk), f32),
            pltpu.VMEM((4, rows, chunk), f32),
            dma((3, heads, 8)), dma((3, heads, 8)), dma((3, heads)),
            dma((7, 2)), dma((2, 4, 2)), dma((1,)), dma((8, 2)), dma((2, 4, 2)),
            dma((heads,)), dma((heads,)), dma((2, heads)), dma((2, heads)),
            dma((3, CHUNKS)), dma((3, CHUNKS)), dma((3, CHUNKS)), dma((3, CHUNKS)),
        ],
        compiler_params=pltpu.CompilerParams(
            collective_id=0, has_side_effects=True, vmem_limit_bytes=60 * 1024 * 1024
        ),
    )(
        queries, keys, values, out_weight, residual_in,
        norm_gain.reshape(CHUNKS, 1, chunk), norm_bias.reshape(CHUNKS, 1, chunk),
    )


def solution(mesh):
    in_specs = (
        P(("dp", "ctx"), None),
        P(("dp", "ctx"), None),
        P(("dp", "ctx"), None),
        P(("dp", "ctx"), None),
        P("ctx", "dp"),
        P(),
        P(),
    )
    out_specs = P(("dp", "ctx"), None)
    fused = mesh.shape["dp"] == 4 and mesh.shape["ctx"] == 8
    local = local_fused if fused else local_general
    return jax.shard_map(local, mesh=mesh, in_specs=in_specs, out_specs=out_specs, check_vma=False)
```

```python
import math

import jax
import jax.numpy as jnp
from jax import lax
from jax.experimental import pallas as pl
from jax.experimental.pallas import tpu as pltpu
from jax.sharding import PartitionSpec as P

HEADS = 32


deepnorm_alpha = 96.0**0.25
norm_eps = 1e-05


def block_rows(length):
    block = min(512, length)
    while length % block != 0:
        block = block + 1
    return block


def attend(all_queries, all_keys, all_values, local_heads):
    length = all_queries.shape[0]
    width = all_queries.shape[1]
    head_dim = width // local_heads
    block = block_rows(length)
    blocks = length // block
    scale = 1.0 / math.sqrt(head_dim)
    query_blocks = all_queries.reshape(blocks, block, local_heads, head_dim)
    key_heads = all_keys.reshape(length, local_heads, head_dim)
    value_heads = all_values.reshape(length, local_heads, head_dim)
    key_position = jnp.arange(length)

    def one_block(inputs):
        number, query_part = inputs
        scores = (
            jnp.einsum("qhd,khd->hqk", query_part, key_heads, preferred_element_type=jnp.float32)
            * scale
        )
        query_position = number * block + jnp.arange(block)
        causal = query_position[:, None] >= key_position[None, :]
        scores = jnp.where(causal[None], scores, -1e30)
        highest = jnp.max(scores, axis=-1, keepdims=True)
        expo = jnp.exp(scores - highest)
        probs = (expo / jnp.sum(expo, axis=-1, keepdims=True)).astype(jnp.bfloat16)
        result = jnp.einsum("hqk,khd->qhd", probs, value_heads, preferred_element_type=jnp.float32)
        return result.astype(jnp.bfloat16).reshape(block, width)

    outputs = lax.map(one_block, (jnp.arange(blocks), query_blocks))
    return outputs.reshape(length, width)


def local_general(queries, keys, values, residual_in, out_weight, norm_gain, norm_bias):
    head_q, head_k, head_v = (
        lax.all_to_all(queries, "ctx", split_axis=1, concat_axis=0, tiled=True),
        lax.all_to_all(keys, "ctx", split_axis=1, concat_axis=0, tiled=True),
        lax.all_to_all(values, "ctx", split_axis=1, concat_axis=0, tiled=True),
    )
    groups = lax.axis_size("ctx")
    attn_heads = attend(head_q, head_k, head_v, HEADS // groups)
    group_rows = lax.all_gather(out_weight, "dp", axis=1, tiled=True)
    summed = lax.psum_scatter(
        jnp.dot(attn_heads, group_rows, preferred_element_type=jnp.float32).astype(jnp.bfloat16),
        "ctx",
        scatter_dimension=0,
        tiled=True,
    )
    attn_float = lax.optimization_barrier(summed).astype(jnp.float32)
    mixed = deepnorm_alpha * residual_in.astype(jnp.float32) + attn_float
    mean = jnp.mean(mixed, axis=-1, keepdims=True)
    centered = mixed - mean
    var = jnp.mean(centered * centered, axis=-1, keepdims=True)
    normed = centered * lax.rsqrt(var + norm_eps) * norm_gain + norm_bias
    return normed.astype(jnp.bfloat16)


MESH = pl.DeviceIdType.MESH
CHUNKS = 8


def fused_kernel(
    q_ref, k_ref, v_ref, w_ref, res_ref, gain_ref, bias_ref, out_ref,
    qh, kh, vh, wf, op, op2, ostage, upr, dnr, stage, own, pbuf,
    s_send, s_recv, s_local, w_send, w_recv, w_local,
    o_send, o_recv, o2_send, o2_recv,
    up_send, up_recv, dn_send, dn_recv,
):
    rows = q_ref.shape[0]
    hd = qh.shape[2]
    heads = qh.shape[0]
    group = heads * hd
    chunk = own.shape[2]
    dp = lax.axis_index("dp")
    ctx = lax.axis_index("ctx")
    xi, core = dp // 2, dp % 2
    zi, yi = ctx // 2, ctx % 2
    sib = (xi * 2 + (1 - core), ctx)
    xnb = ((1 - xi) * 2 + core, ctx)
    ynb = (dp, zi * 2 + (1 - yi))
    is_hub = jnp.logical_and(zi >= 1, zi <= 2)
    is_feeder = jnp.logical_or(zi == 0, zi == 3)
    hub = 1 + zi // 2
    feeder = (zi // 2) * 3

    barrier = pltpu.get_barrier_semaphore()
    for d in range(1, 8):
        pl.semaphore_signal(barrier, inc=1, device_id=(dp, (ctx + d) % 8), device_id_type=MESH)
    for peer in (sib, xnb):
        pl.semaphore_signal(barrier, inc=1, device_id=peer, device_id_type=MESH)
    pl.semaphore_wait(barrier, 9)

    sources = (q_ref, k_ref, v_ref)
    landing = (qh, kh, vh)

    def cols_of(target, h):
        return pl.ds(pl.multiple_of(target * group + h * hd, hd), hd)

    def rows_of(block):
        return pl.ds(pl.multiple_of(block * rows, rows), rows)

    def qkv_copy(a, h, target):
        return pltpu.make_async_remote_copy(
            src_ref=sources[a].at[:, cols_of(target, h)],
            dst_ref=landing[a].at[h, rows_of(ctx), :],
            send_sem=s_send.at[a, h, target],
            recv_sem=s_recv.at[a, h, ctx],
            device_id=(dp, target),
            device_id_type=MESH,
        )

    def qkv_arrival(a, h, source):
        place = landing[a].at[h, rows_of(source), :]
        return pltpu.make_async_remote_copy(
            src_ref=place, dst_ref=place,
            send_sem=s_send.at[a, h, source], recv_sem=s_recv.at[a, h, source],
            device_id=(dp, source), device_id_type=MESH,
        )

    def qkv_local(a, h):
        return pltpu.make_async_copy(
            sources[a].at[:, cols_of(ctx, h)], landing[a].at[h, rows_of(ctx), :], s_local.at[a, h]
        )

    def w_copy(part, slot_y, slot_d, peer, number, first=False):
        place = wf.at[part, slot_y, slot_d]
        return pltpu.make_async_remote_copy(
            src_ref=w_ref.at[:, pl.ds((part % 2) * chunk, chunk)] if first else place,
            dst_ref=place,
            send_sem=w_send.at[number, part],
            recv_sem=w_recv.at[part, slot_y, slot_d],
            device_id=peer,
            device_id_type=MESH,
        )

    xdp = xnb[0]
    routes = {
        0: (yi, dp, xnb),
        1: (yi, dp, ynb),
        2: (yi, dp, sib),
        3: (yi, xdp, sib),
        4: (1 - yi, dp, sib),
        5: (1 - yi, dp, xnb),
        6: (1 - yi, xdp, sib),
    }

    def forward(number, part):
        slot_y, slot_d, peer = routes[number]
        return w_copy(part, slot_y, slot_d, peer, number, number < 3 and part < 2)

    def w_arrive(part, slot_y, slot_d):
        w_copy(part, slot_y, slot_d, ynb, 0).wait_recv()

    def feed_w():
        return w_copy(2, yi, dp, (dp, hub * 2 + yi), 7, True)

    def keep_w(part):
        return pltpu.make_async_copy(
            w_ref.at[:, pl.ds(part * chunk, chunk)], wf.at[part, yi, dp], w_local.at[part]
        )

    for h in range(heads):
        for d in (4, 3, 5, 2, 6, 1, 7):
            for a in range(3):
                qkv_copy(a, h, (ctx + d) % 8).start()
        for a in range(3):
            qkv_local(a, h).start()
        if h == 0 or h == 2:
            forward(h, 1).start()

            @pl.when(is_hub)
            def _():
                forward(h, 0).start()

        if h == 1:
            @pl.when(is_feeder)
            def _():
                feed_w().start()

    forward(1, 1).start()
    for part in range(2):
        keep_w(part).start()

    factor = math.log2(math.e) / math.sqrt(hd)
    block = 2 * rows

    def o_copy(h):
        return pltpu.make_async_remote_copy(
            src_ref=ostage.at[h],
            dst_ref=op.at[yi, h],
            send_sem=o_send.at[h],
            recv_sem=o_recv.at[h],
            device_id=ynb,
            device_id_type=MESH,
        )

    def feed_o(h, same):
        to = yi if same else 1 - yi
        return pltpu.make_async_remote_copy(
            src_ref=op.at[yi, h] if same else ostage.at[h],
            dst_ref=op2.at[yi, h],
            send_sem=o2_send.at[0 if same else 1, h],
            recv_sem=o2_recv.at[yi, h],
            device_id=(dp, hub * 2 + to),
            device_id_type=MESH,
        )

    def one_head(h, carry):
        def arrived(d, inner):
            for a in range(3):
                qkv_arrival(a, h, (ctx + d) % 8).wait_recv()
            return inner

        lax.fori_loop(1, 8, arrived, 0)
        for a in range(3):
            qkv_local(a, h).wait()
        for t in range(4):
            length = block * (t + 1)
            scores = lax.dot_general(
                qh[h, t * block : length, :], kh[h, :length, :],
                (((1,), (1,)), ((), ())), preferred_element_type=jnp.float32,
            )
            at_row = lax.broadcasted_iota(jnp.int32, (block, block), 0)
            at_col = lax.broadcasted_iota(jnp.int32, (block, block), 1)
            diagonal = jnp.where(at_row >= at_col, scores[:, t * block :], -1e30)
            if t > 0:
                scores = jnp.concatenate([scores[:, : t * block], diagonal], axis=1)
            else:
                scores = diagonal
            highest = jnp.max(scores, axis=-1, keepdims=True)
            expo = jnp.exp2((scores - highest) * factor)
            total = jnp.sum(expo, axis=-1, keepdims=True)
            result = jnp.dot(
                expo.astype(jnp.bfloat16), vh[h, :length, :], preferred_element_type=jnp.float32
            ) / total
            low, high = result[:rows], result[rows:]
            mine = jnp.where(yi == 0, low, high)
            theirs = jnp.where(yi == 0, high, low)
            op[yi, h, t * rows : (t + 1) * rows, :] = mine.astype(jnp.bfloat16)
            ostage[h, t * rows : (t + 1) * rows, :] = theirs.astype(jnp.bfloat16)
        o_copy(h).start()

        @pl.when(is_feeder)
        def _():
            feed_o(h, True).start()
            feed_o(h, False).start()

        @pl.when(h == 1)
        def _():
            w_arrive(1, yi, xdp)
            forward(3, 1).start()

            @pl.when(is_hub)
            def _():
                forward(1, 0).start()

        @pl.when(jnp.logical_and(h == 2, is_hub))
        def _():
            w_arrive(0, yi, xdp)
            forward(3, 0).start()
            w_arrive(2, yi, dp)
            forward(0, 2).start()
            forward(2, 2).start()

        return carry

    lax.fori_loop(0, heads, one_head, 0)

    @pl.when(is_hub)
    def _():
        forward(1, 2).start()

    w_arrive(1, 1 - yi, dp)
    forward(5, 1).start()
    forward(4, 1).start()
    for h in range(heads):
        place = op.at[1 - yi, h]
        pltpu.make_async_remote_copy(
            src_ref=place, dst_ref=place, send_sem=o_send.at[h], recv_sem=o_recv.at[h],
            device_id=ynb, device_id_type=MESH,
        ).wait_recv()
    for part in range(2):
        keep_w(part).wait()

    def chain_copy(up, t, c):
        slot = t - 1 if up else t
        to = jnp.minimum(zi + 1, 3) if up else jnp.maximum(zi - 1, 0)
        return pltpu.make_async_remote_copy(
            src_ref=stage.at[slot, c],
            dst_ref=(upr if up else dnr).at[slot, c],
            send_sem=(up_send if up else dn_send).at[slot, c],
            recv_sem=(up_recv if up else dn_recv).at[slot, c],
            device_id=(dp, to * 2 + yi),
            device_id_type=MESH,
        )

    def sends_here(up, t, hubs):
        sends = zi < t if up else zi > t
        if hubs:
            sends = jnp.logical_and(sends, zi >= 1 if up else zi <= 2)
        return sends

    def relay(up, t, c, hubs, allowed):
        slot = t - 1 if up else t
        there = upr if up else dnr
        sends = jnp.logical_and(allowed, sends_here(up, t, hubs))
        first = (1 if hubs else 0) if up else (2 if hubs else 3)

        @pl.when(jnp.logical_and(sends, zi == first))
        def _():
            stage[slot, c] = pbuf[t].astype(jnp.bfloat16)
            chain_copy(up, t, c).start()

        @pl.when(jnp.logical_and(sends, zi != first))
        def _():
            chain_copy(up, t, c).wait_recv()
            stage[slot, c] = (pbuf[t] + there[slot, c].astype(jnp.float32)).astype(jnp.bfloat16)
            chain_copy(up, t, c).start()

    def relays(c, hubs):
        lower, upper = zi < 2, zi >= 2
        ups = (3, 2) if hubs else (3, 2, 1)
        downs = (0, 1) if hubs else (0, 1, 2)
        for t in ups:
            relay(True, t, c, hubs, lower)
        for t in downs:
            relay(False, t, c, hubs, upper)
        for t in ups:
            relay(True, t, c, hubs, upper)
        for t in downs:
            relay(False, t, c, hubs, lower)

    def owner(i):
        return ((xi + i // 2) % 2) * 2 + (core + i) % 2

    def wait_chain(up, slot, c):
        place = (upr if up else dnr).at[slot, c]
        pltpu.make_async_remote_copy(
            src_ref=place, dst_ref=place, send_sem=(up_send if up else dn_send).at[slot, c],
            recv_sem=(up_recv if up else dn_recv).at[slot, c], device_id=ynb, device_id_type=MESH,
        ).wait_recv()

    def finish(i, total):
        for j in (1, 0):
            c = owner(i) * 2 + j

            @pl.when(zi > (1 if j == 0 else 0))
            def _():
                wait_chain(True, zi - 1, c)
                own[c] += upr[zi - 1, c].astype(jnp.float32)

            @pl.when(zi < (2 if j == 0 else 3))
            def _():
                wait_chain(False, zi, c)
                own[c] += dnr[zi, c].astype(jnp.float32)

            res = res_ref[:, pl.ds(pl.multiple_of(c * chunk, 128), chunk)].astype(jnp.float32)
            mixed = deepnorm_alpha * res + own[c].astype(jnp.bfloat16).astype(jnp.float32)
            own[c] = mixed
            total = total + jnp.sum(mixed, axis=-1, keepdims=True)
        return total

    def heads_of(ref):
        return jnp.concatenate([ref[y, h] for y in range(2) for h in range(heads)], axis=1)

    def product(lhs, rhs):
        return jnp.dot(
            lhs, rhs.reshape(2 * group, chunk), preferred_element_type=jnp.float32
        ).reshape(pbuf.shape)

    def one_step(i, total):
        @pl.when(i < 4)
        def _():
            d = owner(i)

            @pl.when(i % 2 == 1)
            def _():
                for y in range(2):
                    w_arrive(1, y, d)

            pbuf[...] = product(heads_of(op), wf[1, :, d])
            relays(d * 2 + 1, False)
            own[d * 2 + 1] = pbuf[zi]

            @pl.when(i == 1)
            def _():
                w_arrive(1, 1 - yi, xdp)
                forward(6, 1).start()

        @pl.when(jnp.logical_and(i == 0, is_hub))
        def _():
            w_arrive(0, 1 - yi, dp)
            forward(5, 0).start()
            forward(4, 0).start()
            w_arrive(2, yi, xdp)
            forward(3, 2).start()

        @pl.when(jnp.logical_and(i == 1, is_hub))
        def _():
            w_arrive(2, 1 - yi, dp)
            forward(5, 2).start()
            forward(4, 2).start()
            for h in range(heads):
                for y in range(2):
                    place = op2.at[y, h]
                    pltpu.make_async_remote_copy(
                        src_ref=place, dst_ref=place, send_sem=o2_send.at[0, h],
                        recv_sem=o2_recv.at[y, h], device_id=ynb, device_id_type=MESH,
                    ).wait_recv()

        @pl.when(jnp.logical_and(i >= 1, is_hub))
        def _():
            d = owner(i - 1)

            @pl.when(i % 2 == 0)
            def _():
                for y in range(2):
                    w_arrive(0, y, d)
                    w_arrive(2, y, d)

            pbuf[...] = product(heads_of(op), wf[0, :, d])
            pbuf[...] += product(heads_of(op2), wf[2, :, d])
            relays(d * 2, True)
            own[d * 2] = pbuf[zi]

            @pl.when(i == 2)
            def _():
                for part in (0, 2):
                    w_arrive(part, 1 - yi, xdp)
                    forward(6, part).start()

        @pl.when(jnp.logical_and(i >= 1, is_feeder))
        def _():
            own[owner(i - 1) * 2] = jnp.zeros(own.shape[1:], jnp.float32)

        return lax.cond(i > 1, lambda: finish(i - 2, total), lambda: total)

    total = lax.fori_loop(0, 5, one_step, jnp.zeros((rows, 1), jnp.float32))
    total = finish(3, total)

    width = chunk * CHUNKS
    mean = total / width
    squares = jnp.zeros((rows, 1), jnp.float32)
    for c in range(CHUNKS):
        centered = own[c] - mean
        squares += jnp.sum(centered * centered, axis=-1, keepdims=True)
    inverse = lax.rsqrt(squares / width + norm_eps)
    for c in range(CHUNKS):
        normed = (own[c] - mean) * inverse * gain_ref[c] + bias_ref[c]
        out_ref[:, c * chunk : (c + 1) * chunk] = normed.astype(out_ref.dtype)

    def sent_qkv(h, carry):
        def sent(d, inner):
            for a in range(3):
                qkv_copy(a, h, (ctx + d) % 8).wait_send()
            return inner

        lax.fori_loop(1, 8, sent, 0)
        o_copy(h).wait_send()

        @pl.when(is_feeder)
        def _():
            feed_o(h, True).wait_send()
            feed_o(h, False).wait_send()

        return carry

    lax.fori_loop(0, heads, sent_qkv, 0)
    for number in routes:
        forward(number, 1).wait_send()

    @pl.when(is_feeder)
    def _():
        feed_w().wait_send()

    @pl.when(is_hub)
    def _():
        for number in routes:
            for part in (0, 2):
                forward(number, part).wait_send()

    def sent_chain(d, carry):
        for j in range(2):
            for up, targets in ((True, (3, 2, 1)), (False, (0, 1, 2))):
                for t in targets:
                    @pl.when(sends_here(up, t, j == 0))
                    def _():
                        chain_copy(up, t, d * 2 + j).wait_send()
        return carry

    lax.fori_loop(0, CHUNKS // 2, sent_chain, 0)


def local_fused(queries, keys, values, residual_in, out_weight, norm_gain, norm_bias):
    rows, width = residual_in.shape
    group, columns = out_weight.shape
    hd = queries.shape[1] // HEADS
    heads = group // hd
    length = rows * 8
    chunk = width // CHUNKS
    bf16, f32 = jnp.bfloat16, jnp.float32
    dma = pltpu.SemaphoreType.DMA
    in_vmem = pl.BlockSpec(memory_space=pltpu.VMEM)
    in_any = pl.BlockSpec(memory_space=pl.ANY)
    return pl.pallas_call(
        fused_kernel,
        out_shape=jax.ShapeDtypeStruct((rows, width), bf16),
        in_specs=[in_any] * 4 + [in_vmem] * 3,
        out_specs=in_vmem,
        scratch_shapes=[
            pltpu.VMEM((heads, length, hd), bf16),
            pltpu.VMEM((heads, length, hd), bf16),
            pltpu.VMEM((heads, length, hd), bf16),
            pltpu.VMEM((3, 2, 4, group, chunk), bf16),
            pltpu.VMEM((2, heads, length // 2, hd), bf16),
            pltpu.VMEM((2, heads, length // 2, hd), bf16),
            pltpu.VMEM((heads, length // 2, hd), bf16),
            pltpu.VMEM((3, CHUNKS, rows, chunk), bf16),
            pltpu.VMEM((3, CHUNKS, rows, chunk), bf16),
            pltpu.VMEM((3, CHUNKS, rows, chunk), bf16),
            pltpu.VMEM((CHUNKS, rows, chunk), f32),
            pltpu.VMEM((4, rows, chunk), f32),
            dma((3, heads, 8)), dma((3, heads, 8)), dma((3, heads)),
            dma((8, 3)), dma((3, 2, 4)), dma((2,)),
            dma((heads,)), dma((heads,)), dma((2, heads)), dma((2, heads)),
            dma((3, CHUNKS)), dma((3, CHUNKS)), dma((3, CHUNKS)), dma((3, CHUNKS)),
        ],
        compiler_params=pltpu.CompilerParams(
            collective_id=0, has_side_effects=True, vmem_limit_bytes=60 * 1024 * 1024
        ),
    )(
        queries, keys, values, out_weight, residual_in,
        norm_gain.reshape(CHUNKS, 1, chunk), norm_bias.reshape(CHUNKS, 1, chunk),
    )


def solution(mesh):
    in_specs = (
        P(("dp", "ctx"), None),
        P(("dp", "ctx"), None),
        P(("dp", "ctx"), None),
        P(("dp", "ctx"), None),
        P("ctx", "dp"),
        P(),
        P(),
    )
    out_specs = P(("dp", "ctx"), None)
    fused = mesh.shape["dp"] == 4 and mesh.shape["ctx"] == 8
    local = local_fused if fused else local_general
    return jax.shard_map(local, mesh=mesh, in_specs=in_specs, out_specs=out_specs, check_vma=False)
```

```python
import math

import jax
import jax.numpy as jnp
from jax import lax
from jax.experimental import pallas as pl
from jax.experimental.pallas import tpu as pltpu
from jax.sharding import PartitionSpec as P

HEADS = 32


deepnorm_alpha = 96.0**0.25
norm_eps = 1e-05


def block_rows(length):
    block = min(512, length)
    while length % block != 0:
        block = block + 1
    return block


def attend(all_queries, all_keys, all_values, local_heads):
    length = all_queries.shape[0]
    width = all_queries.shape[1]
    head_dim = width // local_heads
    block = block_rows(length)
    blocks = length // block
    scale = 1.0 / math.sqrt(head_dim)
    query_blocks = all_queries.reshape(blocks, block, local_heads, head_dim)
    key_heads = all_keys.reshape(length, local_heads, head_dim)
    value_heads = all_values.reshape(length, local_heads, head_dim)
    key_position = jnp.arange(length)

    def one_block(inputs):
        number, query_part = inputs
        scores = (
            jnp.einsum("qhd,khd->hqk", query_part, key_heads, preferred_element_type=jnp.float32)
            * scale
        )
        query_position = number * block + jnp.arange(block)
        causal = query_position[:, None] >= key_position[None, :]
        scores = jnp.where(causal[None], scores, -1e30)
        highest = jnp.max(scores, axis=-1, keepdims=True)
        expo = jnp.exp(scores - highest)
        probs = (expo / jnp.sum(expo, axis=-1, keepdims=True)).astype(jnp.bfloat16)
        result = jnp.einsum("hqk,khd->qhd", probs, value_heads, preferred_element_type=jnp.float32)
        return result.astype(jnp.bfloat16).reshape(block, width)

    outputs = lax.map(one_block, (jnp.arange(blocks), query_blocks))
    return outputs.reshape(length, width)


def local_general(queries, keys, values, residual_in, out_weight, norm_gain, norm_bias):
    head_q, head_k, head_v = (
        lax.all_to_all(queries, "ctx", split_axis=1, concat_axis=0, tiled=True),
        lax.all_to_all(keys, "ctx", split_axis=1, concat_axis=0, tiled=True),
        lax.all_to_all(values, "ctx", split_axis=1, concat_axis=0, tiled=True),
    )
    groups = lax.axis_size("ctx")
    attn_heads = attend(head_q, head_k, head_v, HEADS // groups)
    group_rows = lax.all_gather(out_weight, "dp", axis=1, tiled=True)
    summed = lax.psum_scatter(
        jnp.dot(attn_heads, group_rows, preferred_element_type=jnp.float32).astype(jnp.bfloat16),
        "ctx",
        scatter_dimension=0,
        tiled=True,
    )
    attn_float = lax.optimization_barrier(summed).astype(jnp.float32)
    mixed = deepnorm_alpha * residual_in.astype(jnp.float32) + attn_float
    mean = jnp.mean(mixed, axis=-1, keepdims=True)
    centered = mixed - mean
    var = jnp.mean(centered * centered, axis=-1, keepdims=True)
    normed = centered * lax.rsqrt(var + norm_eps) * norm_gain + norm_bias
    return normed.astype(jnp.bfloat16)


MESH = pl.DeviceIdType.MESH


def fused_kernel(
    q_ref, k_ref, v_ref, w_ref, res_ref, gain_ref, bias_ref, out_ref,
    qh, kh, vh, wf_hub, wf_chain, op, op2, ostage,
    upr_hub, dnr_hub, stage_hub, own_hub, pbuf_hub,
    upr_chain, dnr_chain, stage_chain, own_chain, pbuf_chain,
    s_send, s_recv, s_local, w_send, w_recv, w_local,
    o_send, o_recv, o2_send, o2_recv,
    up_send, up_recv, dn_send, dn_recv,
):
    rows = q_ref.shape[0]
    hd = qh.shape[2]
    heads = qh.shape[0]
    group = heads * hd
    columns = w_ref.shape[1]
    chunks = (own_hub.shape[2], own_chain.shape[2])
    starts = (0, chunks[0])
    uprs, dnrs = (upr_hub, upr_chain), (dnr_hub, dnr_chain)
    stages, owns = (stage_hub, stage_chain), (own_hub, own_chain)
    pbufs = (pbuf_hub, pbuf_chain)
    dp = lax.axis_index("dp")
    ctx = lax.axis_index("ctx")
    xi, core = dp // 2, dp % 2
    zi, yi = ctx // 2, ctx % 2
    sib = (xi * 2 + (1 - core), ctx)
    xnb = ((1 - xi) * 2 + core, ctx)
    ynb = (dp, zi * 2 + (1 - yi))
    is_hub = jnp.logical_and(zi >= 1, zi <= 2)
    is_feeder = jnp.logical_or(zi == 0, zi == 3)
    hub = 1 + zi // 2
    feeder = (zi // 2) * 3

    barrier = pltpu.get_barrier_semaphore()
    for d in range(1, 8):
        pl.semaphore_signal(barrier, inc=1, device_id=(dp, (ctx + d) % 8), device_id_type=MESH)
    for peer in (sib, xnb):
        pl.semaphore_signal(barrier, inc=1, device_id=peer, device_id_type=MESH)
    pl.semaphore_wait(barrier, 9)

    sources = (q_ref, k_ref, v_ref)
    landing = (qh, kh, vh)

    def cols_of(target, h):
        return pl.ds(pl.multiple_of(target * group + h * hd, hd), hd)

    def rows_of(block):
        return pl.ds(pl.multiple_of(block * rows, rows), rows)

    def qkv_copy(a, h, target):
        return pltpu.make_async_remote_copy(
            src_ref=sources[a].at[:, cols_of(target, h)],
            dst_ref=landing[a].at[h, rows_of(ctx), :],
            send_sem=s_send.at[a, h, target],
            recv_sem=s_recv.at[a, h, ctx],
            device_id=(dp, target),
            device_id_type=MESH,
        )

    def qkv_arrival(a, h, source):
        place = landing[a].at[h, rows_of(source), :]
        return pltpu.make_async_remote_copy(
            src_ref=place, dst_ref=place,
            send_sem=s_send.at[a, h, source], recv_sem=s_recv.at[a, h, source],
            device_id=(dp, source), device_id_type=MESH,
        )

    def qkv_local(a, h):
        return pltpu.make_async_copy(
            sources[a].at[:, cols_of(ctx, h)], landing[a].at[h, rows_of(ctx), :], s_local.at[a, h]
        )

    def w_place(part, slot_y, slot_d):
        return wf_chain.at[slot_y, slot_d] if part == 1 else wf_hub.at[part // 2, slot_y, slot_d]

    def w_copy(part, slot_y, slot_d, peer, number, first=False):
        place = w_place(part, slot_y, slot_d)
        return pltpu.make_async_remote_copy(
            src_ref=w_ref.at[:, pl.ds(starts[part % 2], chunks[part % 2])] if first else place,
            dst_ref=place,
            send_sem=w_send.at[number, part],
            recv_sem=w_recv.at[part, slot_y, slot_d],
            device_id=peer,
            device_id_type=MESH,
        )

    xdp = xnb[0]
    routes = {
        0: (yi, dp, xnb),
        1: (yi, dp, ynb),
        2: (yi, dp, sib),
        3: (yi, xdp, sib),
        4: (1 - yi, dp, sib),
        5: (1 - yi, dp, xnb),
        6: (1 - yi, xdp, sib),
    }

    def forward(number, part):
        slot_y, slot_d, peer = routes[number]
        return w_copy(part, slot_y, slot_d, peer, number, number < 3 and part < 2)

    def w_arrive(part, slot_y, slot_d):
        w_copy(part, slot_y, slot_d, ynb, 0).wait_recv()

    def feed_w():
        return w_copy(2, yi, dp, (dp, hub * 2 + yi), 7, True)

    def keep_w(part):
        return pltpu.make_async_copy(
            w_ref.at[:, pl.ds(starts[part], chunks[part])], w_place(part, yi, dp), w_local.at[part]
        )

    for h in range(heads):
        for d in (4, 3, 5, 2, 6, 1, 7):
            for a in range(3):
                qkv_copy(a, h, (ctx + d) % 8).start()
        for a in range(3):
            qkv_local(a, h).start()
        if h == 0 or h == 2:
            forward(h, 1).start()

            @pl.when(is_hub)
            def _():
                forward(h, 0).start()

        if h == 1:
            forward(1, 1).start()

            @pl.when(is_feeder)
            def _():
                feed_w().start()

    for part in range(2):
        keep_w(part).start()

    factor = math.log2(math.e) / math.sqrt(hd)
    block = 2 * rows

    def o_copy(h):
        return pltpu.make_async_remote_copy(
            src_ref=ostage.at[h],
            dst_ref=op.at[yi, h],
            send_sem=o_send.at[h],
            recv_sem=o_recv.at[h],
            device_id=ynb,
            device_id_type=MESH,
        )

    def feed_o(h, y):
        return pltpu.make_async_remote_copy(
            src_ref=op.at[y, h],
            dst_ref=op2.at[y, h],
            send_sem=o2_send.at[y, h],
            recv_sem=o2_recv.at[y, h],
            device_id=(dp, hub * 2 + yi),
            device_id_type=MESH,
        )

    def other_half(h):
        place = op.at[1 - yi, h]
        pltpu.make_async_remote_copy(
            src_ref=place, dst_ref=place, send_sem=o_send.at[h], recv_sem=o_recv.at[h],
            device_id=ynb, device_id_type=MESH,
        ).wait_recv()

        @pl.when(is_feeder)
        def _():
            feed_o(h, 1 - yi).start()

    def one_head(h, carry):
        def arrived(d, inner):
            for a in range(3):
                qkv_arrival(a, h, (ctx + d) % 8).wait_recv()
            return inner

        lax.fori_loop(1, 8, arrived, 0)
        for a in range(3):
            qkv_local(a, h).wait()
        for t in range(4):
            length = block * (t + 1)
            scores = lax.dot_general(
                qh[h, t * block : length, :], kh[h, :length, :],
                (((1,), (1,)), ((), ())), preferred_element_type=jnp.float32,
            )
            at_row = lax.broadcasted_iota(jnp.int32, (block, block), 0)
            at_col = lax.broadcasted_iota(jnp.int32, (block, block), 1)
            diagonal = jnp.where(at_row >= at_col, scores[:, t * block :], -1e30)
            if t > 0:
                scores = jnp.concatenate([scores[:, : t * block], diagonal], axis=1)
            else:
                scores = diagonal
            highest = jnp.max(scores, axis=-1, keepdims=True)
            expo = jnp.exp2((scores - highest) * factor)
            total = jnp.sum(expo, axis=-1, keepdims=True)
            result = jnp.dot(
                expo.astype(jnp.bfloat16), vh[h, :length, :], preferred_element_type=jnp.float32
            ) / total
            low, high = result[:rows], result[rows:]
            mine = jnp.where(yi == 0, low, high)
            theirs = jnp.where(yi == 0, high, low)
            op[yi, h, t * rows : (t + 1) * rows, :] = mine.astype(jnp.bfloat16)
            ostage[h, t * rows : (t + 1) * rows, :] = theirs.astype(jnp.bfloat16)
        o_copy(h).start()

        @pl.when(is_feeder)
        def _():
            feed_o(h, yi).start()

        @pl.when(h > 0)
        def _():
            other_half(h - 1)

        @pl.when(h == 1)
        def _():
            w_arrive(1, yi, xdp)
            forward(3, 1).start()

            @pl.when(is_hub)
            def _():
                forward(1, 0).start()

        @pl.when(jnp.logical_and(h == 2, is_hub))
        def _():
            w_arrive(0, yi, xdp)
            forward(3, 0).start()
            w_arrive(2, yi, dp)
            forward(0, 2).start()
            forward(2, 2).start()

        return carry

    lax.fori_loop(0, heads, one_head, 0)

    @pl.when(is_hub)
    def _():
        forward(1, 2).start()

    w_arrive(1, 1 - yi, dp)
    forward(5, 1).start()
    forward(4, 1).start()
    other_half(heads - 1)
    for part in range(2):
        keep_w(part).wait()

    def chain_copy(up, t, j, d):
        slot = t - 1 if up else t
        to = jnp.minimum(zi + 1, 3) if up else jnp.maximum(zi - 1, 0)
        return pltpu.make_async_remote_copy(
            src_ref=stages[j].at[slot, d],
            dst_ref=(uprs if up else dnrs)[j].at[slot, d],
            send_sem=(up_send if up else dn_send).at[slot, d * 2 + j],
            recv_sem=(up_recv if up else dn_recv).at[slot, d * 2 + j],
            device_id=(dp, to * 2 + yi),
            device_id_type=MESH,
        )

    def sends_here(up, t, hubs):
        sends = zi < t if up else zi > t
        if hubs:
            sends = jnp.logical_and(sends, zi >= 1 if up else zi <= 2)
        return sends

    def relay(up, t, j, d, allowed):
        hubs = j == 0
        slot = t - 1 if up else t
        there, stage, pbuf = (uprs if up else dnrs)[j], stages[j], pbufs[j]
        sends = jnp.logical_and(allowed, sends_here(up, t, hubs))
        first = (1 if hubs else 0) if up else (2 if hubs else 3)

        @pl.when(jnp.logical_and(sends, zi == first))
        def _():
            stage[slot, d] = pbuf[t].astype(jnp.bfloat16)
            chain_copy(up, t, j, d).start()

        @pl.when(jnp.logical_and(sends, zi != first))
        def _():
            chain_copy(up, t, j, d).wait_recv()
            stage[slot, d] = (pbuf[t] + there[slot, d].astype(jnp.float32)).astype(jnp.bfloat16)
            chain_copy(up, t, j, d).start()

    def relays(j, d):
        hubs = j == 0
        lower, upper = zi < 2, zi >= 2
        ups = (3, 2) if hubs else (3, 2, 1)
        downs = (0, 1) if hubs else (0, 1, 2)
        for t in ups:
            relay(True, t, j, d, lower)
        for t in downs:
            relay(False, t, j, d, upper)
        for t in ups:
            relay(True, t, j, d, upper)
        for t in downs:
            relay(False, t, j, d, lower)

    def owner(i):
        return ((xi + i // 2) % 2) * 2 + (core + i) % 2

    def wait_chain(up, slot, j, d):
        place = (uprs if up else dnrs)[j].at[slot, d]
        at = d * 2 + j
        pltpu.make_async_remote_copy(
            src_ref=place, dst_ref=place, send_sem=(up_send if up else dn_send).at[slot, at],
            recv_sem=(up_recv if up else dn_recv).at[slot, at], device_id=ynb, device_id_type=MESH,
        ).wait_recv()

    def finish(i, total):
        d = owner(i)
        for j in (1, 0):
            own = owns[j]

            @pl.when(zi > (1 if j == 0 else 0))
            def _():
                wait_chain(True, zi - 1, j, d)
                own[d] += uprs[j][zi - 1, d].astype(jnp.float32)

            @pl.when(zi < (2 if j == 0 else 3))
            def _():
                wait_chain(False, zi, j, d)
                own[d] += dnrs[j][zi, d].astype(jnp.float32)

            cols = pl.ds(pl.multiple_of(d * columns + starts[j], 128), chunks[j])
            res = res_ref[:, cols].astype(jnp.float32)
            mixed = deepnorm_alpha * res + own[d].astype(jnp.bfloat16).astype(jnp.float32)
            own[d] = mixed
            total = total + jnp.sum(mixed, axis=-1, keepdims=True)
        return total

    def heads_of(ref):
        return jnp.concatenate([ref[y, h] for y in range(2) for h in range(heads)], axis=1)

    def product(lhs, rhs):
        wide = rhs.shape[-1]
        return jnp.dot(
            lhs, rhs.reshape(2 * group, wide), preferred_element_type=jnp.float32
        ).reshape(4, rows, wide)

    def one_step(i, total):
        d = owner(i)

        @pl.when(i % 2 == 1)
        def _():
            for y in range(2):
                w_arrive(1, y, d)

        pbuf_chain[...] = product(heads_of(op), wf_chain[:, d])
        relays(1, d)
        own_chain[d] = pbuf_chain[zi]

        @pl.when(i == 1)
        def _():
            w_arrive(1, 1 - yi, xdp)
            forward(6, 1).start()

        @pl.when(jnp.logical_and(i == 0, is_hub))
        def _():
            w_arrive(0, 1 - yi, dp)
            forward(5, 0).start()
            forward(4, 0).start()
            w_arrive(2, yi, xdp)
            forward(3, 2).start()
            w_arrive(2, 1 - yi, dp)
            forward(5, 2).start()
            forward(4, 2).start()
            for h in range(heads):
                for y in range(2):
                    place = op2.at[y, h]
                    pltpu.make_async_remote_copy(
                        src_ref=place, dst_ref=place, send_sem=o2_send.at[0, h],
                        recv_sem=o2_recv.at[y, h], device_id=ynb, device_id_type=MESH,
                    ).wait_recv()

        @pl.when(is_hub)
        def _():
            @pl.when(i % 2 == 1)
            def _():
                for y in range(2):
                    w_arrive(0, y, d)
                    w_arrive(2, y, d)

            pbuf_hub[...] = product(heads_of(op), wf_hub[0, :, d])
            pbuf_hub[...] += product(heads_of(op2), wf_hub[1, :, d])
            relays(0, d)
            own_hub[d] = pbuf_hub[zi]

            @pl.when(i == 1)
            def _():
                for part in (0, 2):
                    w_arrive(part, 1 - yi, xdp)
                    forward(6, part).start()

        @pl.when(is_feeder)
        def _():
            own_hub[d] = jnp.zeros(own_hub.shape[1:], jnp.float32)

        return lax.cond(i > 0, lambda: finish(i - 1, total), lambda: total)

    total = lax.fori_loop(0, 4, one_step, jnp.zeros((rows, 1), jnp.float32))
    total = finish(3, total)

    width = columns * 4
    mean = total / width
    squares = jnp.zeros((rows, 1), jnp.float32)
    for own in owns:
        for d in range(4):
            centered = own[d] - mean
            squares += jnp.sum(centered * centered, axis=-1, keepdims=True)
    inverse = lax.rsqrt(squares / width + norm_eps)
    for j, own in enumerate(owns):
        for d in range(4):
            low = d * columns + starts[j]
            cols = slice(low, low + chunks[j])
            normed = (own[d] - mean) * inverse * gain_ref[:, cols] + bias_ref[:, cols]
            out_ref[:, cols] = normed.astype(out_ref.dtype)

    def sent_qkv(h, carry):
        def sent(d, inner):
            for a in range(3):
                qkv_copy(a, h, (ctx + d) % 8).wait_send()
            return inner

        lax.fori_loop(1, 8, sent, 0)
        o_copy(h).wait_send()

        @pl.when(is_feeder)
        def _():
            feed_o(h, 0).wait_send()
            feed_o(h, 1).wait_send()

        return carry

    lax.fori_loop(0, heads, sent_qkv, 0)
    for number in routes:
        forward(number, 1).wait_send()

    @pl.when(is_feeder)
    def _():
        feed_w().wait_send()

    @pl.when(is_hub)
    def _():
        for number in routes:
            for part in (0, 2):
                forward(number, part).wait_send()

    def sent_chain(d, carry):
        for j in range(2):
            for up, targets in ((True, (3, 2, 1)), (False, (0, 1, 2))):
                for t in targets:
                    @pl.when(sends_here(up, t, j == 0))
                    def _():
                        chain_copy(up, t, j, d).wait_send()
        return carry

    lax.fori_loop(0, 4, sent_chain, 0)


def local_fused(queries, keys, values, residual_in, out_weight, norm_gain, norm_bias):
    rows, width = residual_in.shape
    group, columns = out_weight.shape
    hd = queries.shape[1] // HEADS
    heads = group // hd
    length = rows * 8
    hub_part = columns // 7 * 4
    chain_part = columns - hub_part
    bf16, f32 = jnp.bfloat16, jnp.float32
    dma = pltpu.SemaphoreType.DMA
    in_vmem = pl.BlockSpec(memory_space=pltpu.VMEM)
    in_any = pl.BlockSpec(memory_space=pl.ANY)
    return pl.pallas_call(
        fused_kernel,
        out_shape=jax.ShapeDtypeStruct((rows, width), bf16),
        in_specs=[in_any] * 4 + [in_vmem] * 3,
        out_specs=in_vmem,
        scratch_shapes=[
            pltpu.VMEM((heads, length, hd), bf16),
            pltpu.VMEM((heads, length, hd), bf16),
            pltpu.VMEM((heads, length, hd), bf16),
            pltpu.VMEM((2, 2, 4, group, hub_part), bf16),
            pltpu.VMEM((2, 4, group, chain_part), bf16),
            pltpu.VMEM((2, heads, length // 2, hd), bf16),
            pltpu.VMEM((2, heads, length // 2, hd), bf16),
            pltpu.VMEM((heads, length // 2, hd), bf16),
        ] + [
            pltpu.VMEM(shape + (rows, part), kind)
            for part in (hub_part, chain_part)
            for shape, kind in (((3, 4), bf16),) * 3 + (((4,), f32),) * 2
        ] + [
            dma((3, heads, 8)), dma((3, heads, 8)), dma((3, heads)),
            dma((8, 3)), dma((3, 2, 4)), dma((2,)),
            dma((heads,)), dma((heads,)), dma((2, heads)), dma((2, heads)),
            dma((3, 8)), dma((3, 8)), dma((3, 8)), dma((3, 8)),
        ],
        compiler_params=pltpu.CompilerParams(
            collective_id=0, has_side_effects=True, vmem_limit_bytes=60 * 1024 * 1024
        ),
    )(
        queries, keys, values, out_weight, residual_in,
        norm_gain.reshape(1, width), norm_bias.reshape(1, width),
    )


def solution(mesh):
    in_specs = (
        P(("dp", "ctx"), None),
        P(("dp", "ctx"), None),
        P(("dp", "ctx"), None),
        P(("dp", "ctx"), None),
        P("ctx", "dp"),
        P(),
        P(),
    )
    out_specs = P(("dp", "ctx"), None)
    fused = mesh.shape["dp"] == 4 and mesh.shape["ctx"] == 8
    local = local_fused if fused else local_general
    return jax.shard_map(local, mesh=mesh, in_specs=in_specs, out_specs=out_specs, check_vma=False)
```

```python
import math

import jax
import jax.numpy as jnp
from jax import lax
from jax.experimental import pallas as pl
from jax.experimental.pallas import tpu as pltpu
from jax.sharding import PartitionSpec as P

HEADS = 32


deepnorm_alpha = 96.0**0.25
norm_eps = 1e-05


def block_rows(length):
    block = min(512, length)
    while length % block != 0:
        block = block + 1
    return block


def attend(all_queries, all_keys, all_values, local_heads):
    length = all_queries.shape[0]
    width = all_queries.shape[1]
    head_dim = width // local_heads
    block = block_rows(length)
    blocks = length // block
    scale = 1.0 / math.sqrt(head_dim)
    query_blocks = all_queries.reshape(blocks, block, local_heads, head_dim)
    key_heads = all_keys.reshape(length, local_heads, head_dim)
    value_heads = all_values.reshape(length, local_heads, head_dim)
    key_position = jnp.arange(length)

    def one_block(inputs):
        number, query_part = inputs
        scores = (
            jnp.einsum("qhd,khd->hqk", query_part, key_heads, preferred_element_type=jnp.float32)
            * scale
        )
        query_position = number * block + jnp.arange(block)
        causal = query_position[:, None] >= key_position[None, :]
        scores = jnp.where(causal[None], scores, -1e30)
        highest = jnp.max(scores, axis=-1, keepdims=True)
        expo = jnp.exp(scores - highest)
        probs = (expo / jnp.sum(expo, axis=-1, keepdims=True)).astype(jnp.bfloat16)
        result = jnp.einsum("hqk,khd->qhd", probs, value_heads, preferred_element_type=jnp.float32)
        return result.astype(jnp.bfloat16).reshape(block, width)

    outputs = lax.map(one_block, (jnp.arange(blocks), query_blocks))
    return outputs.reshape(length, width)


def local_general(queries, keys, values, residual_in, out_weight, norm_gain, norm_bias):
    head_q, head_k, head_v = (
        lax.all_to_all(queries, "ctx", split_axis=1, concat_axis=0, tiled=True),
        lax.all_to_all(keys, "ctx", split_axis=1, concat_axis=0, tiled=True),
        lax.all_to_all(values, "ctx", split_axis=1, concat_axis=0, tiled=True),
    )
    groups = lax.axis_size("ctx")
    attn_heads = attend(head_q, head_k, head_v, HEADS // groups)
    group_rows = lax.all_gather(out_weight, "dp", axis=1, tiled=True)
    summed = lax.psum_scatter(
        jnp.dot(attn_heads, group_rows, preferred_element_type=jnp.float32).astype(jnp.bfloat16),
        "ctx",
        scatter_dimension=0,
        tiled=True,
    )
    attn_float = lax.optimization_barrier(summed).astype(jnp.float32)
    mixed = deepnorm_alpha * residual_in.astype(jnp.float32) + attn_float
    mean = jnp.mean(mixed, axis=-1, keepdims=True)
    centered = mixed - mean
    var = jnp.mean(centered * centered, axis=-1, keepdims=True)
    normed = centered * lax.rsqrt(var + norm_eps) * norm_gain + norm_bias
    return normed.astype(jnp.bfloat16)


MESH = pl.DeviceIdType.MESH


def fused_kernel(
    q_ref, k_ref, v_ref, w_ref, res_ref, gain_ref, bias_ref, out_ref,
    qh, kh, vh, wf_hub, wf_chain, op, op2, ostage,
    upr_hub, dnr_hub, stage_hub, own_hub, pbuf_hub,
    upr_chain, dnr_chain, stage_chain, own_chain, pbuf_chain,
    s_send, s_recv, s_local, w_send, w_recv, w_local,
    o_send, o_recv, o2_send, o2_recv,
    up_send, up_recv, dn_send, dn_recv,
):
    rows = q_ref.shape[0]
    hd = qh.shape[2]
    heads = qh.shape[0]
    group = heads * hd
    columns = w_ref.shape[1]
    chunks = (own_hub.shape[2], own_chain.shape[2])
    starts = (0, chunks[0])
    uprs, dnrs = (upr_hub, upr_chain), (dnr_hub, dnr_chain)
    stages, owns = (stage_hub, stage_chain), (own_hub, own_chain)
    pbufs = (pbuf_hub, pbuf_chain)
    dp = lax.axis_index("dp")
    ctx = lax.axis_index("ctx")
    xi, core = dp // 2, dp % 2
    zi, yi = ctx // 2, ctx % 2
    sib = (xi * 2 + (1 - core), ctx)
    xnb = ((1 - xi) * 2 + core, ctx)
    ynb = (dp, zi * 2 + (1 - yi))
    is_hub = jnp.logical_and(zi >= 1, zi <= 2)
    is_feeder = jnp.logical_or(zi == 0, zi == 3)
    hub = 1 + zi // 2
    feeder = (zi // 2) * 3

    barrier = pltpu.get_barrier_semaphore()
    for d in range(1, 8):
        pl.semaphore_signal(barrier, inc=1, device_id=(dp, (ctx + d) % 8), device_id_type=MESH)
    for peer in (sib, xnb):
        pl.semaphore_signal(barrier, inc=1, device_id=peer, device_id_type=MESH)
    pl.semaphore_wait(barrier, 9)

    sources = (q_ref, k_ref, v_ref)
    landing = (qh, kh, vh)

    def cols_of(target, h):
        return pl.ds(pl.multiple_of(target * group + h * hd, hd), hd)

    def rows_of(block):
        return pl.ds(pl.multiple_of(block * rows, rows), rows)

    def qkv_copy(a, h, target):
        return pltpu.make_async_remote_copy(
            src_ref=sources[a].at[:, cols_of(target, h)],
            dst_ref=landing[a].at[h, rows_of(ctx), :],
            send_sem=s_send.at[a, h, target],
            recv_sem=s_recv.at[a, h, ctx],
            device_id=(dp, target),
            device_id_type=MESH,
        )

    def qkv_arrival(a, h, source):
        place = landing[a].at[h, rows_of(source), :]
        return pltpu.make_async_remote_copy(
            src_ref=place, dst_ref=place,
            send_sem=s_send.at[a, h, source], recv_sem=s_recv.at[a, h, source],
            device_id=(dp, source), device_id_type=MESH,
        )

    def qkv_local(a, h):
        return pltpu.make_async_copy(
            sources[a].at[:, cols_of(ctx, h)], landing[a].at[h, rows_of(ctx), :], s_local.at[a, h]
        )

    def w_place(part, slot_y, slot_d):
        return wf_chain.at[slot_y, slot_d] if part == 1 else wf_hub.at[part // 2, slot_y, slot_d]

    def w_copy(part, slot_y, slot_d, peer, number, first=False):
        place = w_place(part, slot_y, slot_d)
        return pltpu.make_async_remote_copy(
            src_ref=w_ref.at[:, pl.ds(starts[part % 2], chunks[part % 2])] if first else place,
            dst_ref=place,
            send_sem=w_send.at[number, part],
            recv_sem=w_recv.at[part, slot_y, slot_d],
            device_id=peer,
            device_id_type=MESH,
        )

    xdp = xnb[0]
    routes = {
        0: (yi, dp, xnb),
        1: (yi, dp, ynb),
        2: (yi, dp, sib),
        3: (yi, xdp, sib),
        4: (1 - yi, dp, sib),
        5: (1 - yi, dp, xnb),
        6: (1 - yi, xdp, sib),
    }

    def forward(number, part):
        slot_y, slot_d, peer = routes[number]
        return w_copy(part, slot_y, slot_d, peer, number, number < 3 and part < 2)

    def w_arrive(part, slot_y, slot_d):
        w_copy(part, slot_y, slot_d, ynb, 0).wait_recv()

    def feed_w():
        return w_copy(2, yi, dp, (dp, hub * 2 + yi), 7, True)

    def keep_w(part):
        return pltpu.make_async_copy(
            w_ref.at[:, pl.ds(starts[part], chunks[part])], w_place(part, yi, dp), w_local.at[part]
        )

    for h in range(heads):
        for d in (4, 3, 5, 2, 6, 1, 7):
            for a in range(3):
                qkv_copy(a, h, (ctx + d) % 8).start()
        for a in range(3):
            qkv_local(a, h).start()
        if h == 0 or h == 2:
            forward(h, 1).start()

            @pl.when(is_hub)
            def _():
                forward(h, 0).start()

        if h == 1:
            forward(1, 1).start()

            @pl.when(is_feeder)
            def _():
                feed_w().start()

    for part in range(2):
        keep_w(part).start()

    factor = math.log2(math.e) / math.sqrt(hd)
    block = 2 * rows

    def o_copy(h):
        return pltpu.make_async_remote_copy(
            src_ref=ostage.at[h],
            dst_ref=op.at[yi, h],
            send_sem=o_send.at[h],
            recv_sem=o_recv.at[h],
            device_id=ynb,
            device_id_type=MESH,
        )

    def feed_o(h, y):
        return pltpu.make_async_remote_copy(
            src_ref=op.at[y, h],
            dst_ref=op2.at[y, h],
            send_sem=o2_send.at[y, h],
            recv_sem=o2_recv.at[y, h],
            device_id=(dp, hub * 2 + yi),
            device_id_type=MESH,
        )

    def other_half(h):
        place = op.at[1 - yi, h]
        pltpu.make_async_remote_copy(
            src_ref=place, dst_ref=place, send_sem=o_send.at[h], recv_sem=o_recv.at[h],
            device_id=ynb, device_id_type=MESH,
        ).wait_recv()

        @pl.when(is_feeder)
        def _():
            feed_o(h, 1 - yi).start()

    def one_head(h, carry):
        def arrived(d, inner):
            for a in range(3):
                qkv_arrival(a, h, (ctx + d) % 8).wait_recv()
            return inner

        lax.fori_loop(1, 8, arrived, 0)
        for a in range(3):
            qkv_local(a, h).wait()
        for t in range(4):
            length = block * (t + 1)
            scores = lax.dot_general(
                qh[h, t * block : length, :], kh[h, :length, :],
                (((1,), (1,)), ((), ())), preferred_element_type=jnp.float32,
            )
            at_row = lax.broadcasted_iota(jnp.int32, (block, block), 0)
            at_col = lax.broadcasted_iota(jnp.int32, (block, block), 1)
            diagonal = jnp.where(at_row >= at_col, scores[:, t * block :], -1e30)
            if t > 0:
                scores = jnp.concatenate([scores[:, : t * block], diagonal], axis=1)
            else:
                scores = diagonal
            highest = jnp.max(scores, axis=-1, keepdims=True)
            expo = jnp.exp2((scores - highest) * factor)
            total = jnp.sum(expo, axis=-1, keepdims=True)
            result = jnp.dot(
                expo.astype(jnp.bfloat16), vh[h, :length, :], preferred_element_type=jnp.float32
            ) / total
            low, high = result[:rows], result[rows:]
            mine = jnp.where(yi == 0, low, high)
            theirs = jnp.where(yi == 0, high, low)
            op[yi, h, t * rows : (t + 1) * rows, :] = mine.astype(jnp.bfloat16)
            ostage[h, t * rows : (t + 1) * rows, :] = theirs.astype(jnp.bfloat16)
        o_copy(h).start()

        @pl.when(is_feeder)
        def _():
            feed_o(h, yi).start()

        @pl.when(h > 0)
        def _():
            other_half(h - 1)

        @pl.when(h == 1)
        def _():
            w_arrive(1, yi, xdp)
            forward(3, 1).start()

            @pl.when(is_hub)
            def _():
                forward(1, 0).start()

        @pl.when(jnp.logical_and(h == 2, is_hub))
        def _():
            w_arrive(0, yi, xdp)
            forward(3, 0).start()
            w_arrive(2, yi, dp)
            forward(0, 2).start()
            forward(2, 2).start()

        return carry

    lax.fori_loop(0, heads, one_head, 0)

    @pl.when(is_hub)
    def _():
        forward(1, 2).start()

    w_arrive(1, 1 - yi, dp)
    forward(5, 1).start()
    forward(4, 1).start()
    other_half(heads - 1)
    for part in range(2):
        keep_w(part).wait()

    def chain_copy(up, t, j, d):
        slot = t - 1 if up else t
        to = jnp.minimum(zi + 1, 3) if up else jnp.maximum(zi - 1, 0)
        return pltpu.make_async_remote_copy(
            src_ref=stages[j].at[slot, d],
            dst_ref=(uprs if up else dnrs)[j].at[slot, d],
            send_sem=(up_send if up else dn_send).at[slot, d * 2 + j],
            recv_sem=(up_recv if up else dn_recv).at[slot, d * 2 + j],
            device_id=(dp, to * 2 + yi),
            device_id_type=MESH,
        )

    def sends_here(up, t, hubs):
        sends = zi < t if up else zi > t
        if hubs:
            sends = jnp.logical_and(sends, zi >= 1 if up else zi <= 2)
        return sends

    def relay(up, t, j, d, allowed):
        hubs = j == 0
        slot = t - 1 if up else t
        there, stage, pbuf = (uprs if up else dnrs)[j], stages[j], pbufs[j]
        sends = jnp.logical_and(allowed, sends_here(up, t, hubs))
        first = (1 if hubs else 0) if up else (2 if hubs else 3)

        @pl.when(jnp.logical_and(sends, zi == first))
        def _():
            stage[slot, d] = pbuf[t].astype(jnp.bfloat16)
            chain_copy(up, t, j, d).start()

        @pl.when(jnp.logical_and(sends, zi != first))
        def _():
            chain_copy(up, t, j, d).wait_recv()
            stage[slot, d] = (pbuf[t] + there[slot, d].astype(jnp.float32)).astype(jnp.bfloat16)
            chain_copy(up, t, j, d).start()

    def relays(j, d):
        hubs = j == 0
        lower, upper = zi < 2, zi >= 2
        ups = (3, 2) if hubs else (3, 2, 1)
        downs = (0, 1) if hubs else (0, 1, 2)
        for t in ups:
            relay(True, t, j, d, lower)
        for t in downs:
            relay(False, t, j, d, upper)
        for t in ups:
            relay(True, t, j, d, upper)
        for t in downs:
            relay(False, t, j, d, lower)

    def owner(i):
        return ((xi + i // 2) % 2) * 2 + (core + i) % 2

    def wait_chain(up, slot, j, d):
        place = (uprs if up else dnrs)[j].at[slot, d]
        at = d * 2 + j
        pltpu.make_async_remote_copy(
            src_ref=place, dst_ref=place, send_sem=(up_send if up else dn_send).at[slot, at],
            recv_sem=(up_recv if up else dn_recv).at[slot, at], device_id=ynb, device_id_type=MESH,
        ).wait_recv()

    def finish(i, total):
        d = owner(i)
        for j in (1, 0):
            own = owns[j]

            @pl.when(zi > (1 if j == 0 else 0))
            def _():
                wait_chain(True, zi - 1, j, d)
                own[d] += uprs[j][zi - 1, d].astype(jnp.float32)

            @pl.when(zi < (2 if j == 0 else 3))
            def _():
                wait_chain(False, zi, j, d)
                own[d] += dnrs[j][zi, d].astype(jnp.float32)

            cols = pl.ds(pl.multiple_of(d * columns + starts[j], 128), chunks[j])
            res = res_ref[:, cols].astype(jnp.float32)
            mixed = deepnorm_alpha * res + own[d].astype(jnp.bfloat16).astype(jnp.float32)
            own[d] = mixed
            total = total + jnp.sum(mixed, axis=-1, keepdims=True)
        return total

    def heads_of(ref):
        return jnp.concatenate([ref[y, h] for y in range(2) for h in range(heads)], axis=1)

    def product(lhs, rhs):
        wide = rhs.shape[-1]
        return jnp.dot(
            lhs, rhs.reshape(2 * group, wide), preferred_element_type=jnp.float32
        ).reshape(4, rows, wide)

    def one_step(i, total):
        @pl.when(i < 4)
        def _():
            d = owner(i)

            @pl.when(i % 2 == 1)
            def _():
                for y in range(2):
                    w_arrive(1, y, d)

            pbuf_chain[...] = product(heads_of(op), wf_chain[:, d])
            relays(1, d)
            own_chain[d] = pbuf_chain[zi]

            @pl.when(i == 1)
            def _():
                w_arrive(1, 1 - yi, xdp)
                forward(6, 1).start()

        @pl.when(jnp.logical_and(i == 0, is_hub))
        def _():
            w_arrive(0, 1 - yi, dp)
            forward(5, 0).start()
            forward(4, 0).start()
            w_arrive(2, yi, xdp)
            forward(3, 2).start()

        @pl.when(jnp.logical_and(i == 1, is_hub))
        def _():
            w_arrive(2, 1 - yi, dp)
            forward(5, 2).start()
            forward(4, 2).start()
            for h in range(heads):
                for y in range(2):
                    place = op2.at[y, h]
                    pltpu.make_async_remote_copy(
                        src_ref=place, dst_ref=place, send_sem=o2_send.at[0, h],
                        recv_sem=o2_recv.at[y, h], device_id=ynb, device_id_type=MESH,
                    ).wait_recv()

        @pl.when(jnp.logical_and(i >= 1, is_hub))
        def _():
            d = owner(i - 1)

            @pl.when(i % 2 == 0)
            def _():
                for y in range(2):
                    w_arrive(0, y, d)
                    w_arrive(2, y, d)

            pbuf_hub[...] = product(heads_of(op), wf_hub[0, :, d])
            pbuf_hub[...] += product(heads_of(op2), wf_hub[1, :, d])
            relays(0, d)
            own_hub[d] = pbuf_hub[zi]

            @pl.when(i == 2)
            def _():
                for part in (0, 2):
                    w_arrive(part, 1 - yi, xdp)
                    forward(6, part).start()

        @pl.when(jnp.logical_and(i >= 1, is_feeder))
        def _():
            own_hub[owner(i - 1)] = jnp.zeros(own_hub.shape[1:], jnp.float32)

        return lax.cond(i > 1, lambda: finish(i - 2, total), lambda: total)

    total = lax.fori_loop(0, 5, one_step, jnp.zeros((rows, 1), jnp.float32))
    total = finish(3, total)

    width = columns * 4
    mean = total / width
    squares = jnp.zeros((rows, 1), jnp.float32)
    for own in owns:
        for d in range(4):
            centered = own[d] - mean
            squares += jnp.sum(centered * centered, axis=-1, keepdims=True)
    inverse = lax.rsqrt(squares / width + norm_eps)
    for j, own in enumerate(owns):
        for d in range(4):
            low = d * columns + starts[j]
            cols = slice(low, low + chunks[j])
            normed = (own[d] - mean) * inverse * gain_ref[:, cols] + bias_ref[:, cols]
            out_ref[:, cols] = normed.astype(out_ref.dtype)

    def sent_qkv(h, carry):
        def sent(d, inner):
            for a in range(3):
                qkv_copy(a, h, (ctx + d) % 8).wait_send()
            return inner

        lax.fori_loop(1, 8, sent, 0)
        o_copy(h).wait_send()

        @pl.when(is_feeder)
        def _():
            feed_o(h, 0).wait_send()
            feed_o(h, 1).wait_send()

        return carry

    lax.fori_loop(0, heads, sent_qkv, 0)
    for number in routes:
        forward(number, 1).wait_send()

    @pl.when(is_feeder)
    def _():
        feed_w().wait_send()

    @pl.when(is_hub)
    def _():
        for number in routes:
            for part in (0, 2):
                forward(number, part).wait_send()

    def sent_chain(d, carry):
        for j in range(2):
            for up, targets in ((True, (3, 2, 1)), (False, (0, 1, 2))):
                for t in targets:
                    @pl.when(sends_here(up, t, j == 0))
                    def _():
                        chain_copy(up, t, j, d).wait_send()
        return carry

    lax.fori_loop(0, 4, sent_chain, 0)


def local_fused(queries, keys, values, residual_in, out_weight, norm_gain, norm_bias):
    rows, width = residual_in.shape
    group, columns = out_weight.shape
    hd = queries.shape[1] // HEADS
    heads = group // hd
    length = rows * 8
    hub_part = columns // 7 * 4
    chain_part = columns - hub_part
    bf16, f32 = jnp.bfloat16, jnp.float32
    dma = pltpu.SemaphoreType.DMA
    in_vmem = pl.BlockSpec(memory_space=pltpu.VMEM)
    in_any = pl.BlockSpec(memory_space=pl.ANY)
    return pl.pallas_call(
        fused_kernel,
        out_shape=jax.ShapeDtypeStruct((rows, width), bf16),
        in_specs=[in_any] * 4 + [in_vmem] * 3,
        out_specs=in_vmem,
        scratch_shapes=[
            pltpu.VMEM((heads, length, hd), bf16),
            pltpu.VMEM((heads, length, hd), bf16),
            pltpu.VMEM((heads, length, hd), bf16),
            pltpu.VMEM((2, 2, 4, group, hub_part), bf16),
            pltpu.VMEM((2, 4, group, chain_part), bf16),
            pltpu.VMEM((2, heads, length // 2, hd), bf16),
            pltpu.VMEM((2, heads, length // 2, hd), bf16),
            pltpu.VMEM((heads, length // 2, hd), bf16),
        ] + [
            pltpu.VMEM(shape + (rows, part), kind)
            for part in (hub_part, chain_part)
            for shape, kind in (((3, 4), bf16),) * 3 + (((4,), f32),) * 2
        ] + [
            dma((3, heads, 8)), dma((3, heads, 8)), dma((3, heads)),
            dma((8, 3)), dma((3, 2, 4)), dma((2,)),
            dma((heads,)), dma((heads,)), dma((2, heads)), dma((2, heads)),
            dma((3, 8)), dma((3, 8)), dma((3, 8)), dma((3, 8)),
        ],
        compiler_params=pltpu.CompilerParams(
            collective_id=0, has_side_effects=True, vmem_limit_bytes=60 * 1024 * 1024
        ),
    )(
        queries, keys, values, out_weight, residual_in,
        norm_gain.reshape(1, width), norm_bias.reshape(1, width),
    )


def solution(mesh):
    in_specs = (
        P(("dp", "ctx"), None),
        P(("dp", "ctx"), None),
        P(("dp", "ctx"), None),
        P(("dp", "ctx"), None),
        P("ctx", "dp"),
        P(),
        P(),
    )
    out_specs = P(("dp", "ctx"), None)
    fused = mesh.shape["dp"] == 4 and mesh.shape["ctx"] == 8
    local = local_fused if fused else local_general
    return jax.shard_map(local, mesh=mesh, in_specs=in_specs, out_specs=out_specs, check_vma=False)
```

```python
import math

import jax
import jax.numpy as jnp
from jax import lax
from jax.experimental import pallas as pl
from jax.experimental.pallas import tpu as pltpu
from jax.sharding import PartitionSpec as P

HEADS = 32


deepnorm_alpha = 96.0**0.25
norm_eps = 1e-05


def block_rows(length):
    block = min(512, length)
    while length % block != 0:
        block = block + 1
    return block


def attend(all_queries, all_keys, all_values, local_heads):
    length = all_queries.shape[0]
    width = all_queries.shape[1]
    head_dim = width // local_heads
    block = block_rows(length)
    blocks = length // block
    scale = 1.0 / math.sqrt(head_dim)
    query_blocks = all_queries.reshape(blocks, block, local_heads, head_dim)
    key_heads = all_keys.reshape(length, local_heads, head_dim)
    value_heads = all_values.reshape(length, local_heads, head_dim)
    key_position = jnp.arange(length)

    def one_block(inputs):
        number, query_part = inputs
        scores = (
            jnp.einsum("qhd,khd->hqk", query_part, key_heads, preferred_element_type=jnp.float32)
            * scale
        )
        query_position = number * block + jnp.arange(block)
        causal = query_position[:, None] >= key_position[None, :]
        scores = jnp.where(causal[None], scores, -1e30)
        highest = jnp.max(scores, axis=-1, keepdims=True)
        expo = jnp.exp(scores - highest)
        probs = (expo / jnp.sum(expo, axis=-1, keepdims=True)).astype(jnp.bfloat16)
        result = jnp.einsum("hqk,khd->qhd", probs, value_heads, preferred_element_type=jnp.float32)
        return result.astype(jnp.bfloat16).reshape(block, width)

    outputs = lax.map(one_block, (jnp.arange(blocks), query_blocks))
    return outputs.reshape(length, width)


def local_general(queries, keys, values, residual_in, out_weight, norm_gain, norm_bias):
    head_q, head_k, head_v = (
        lax.all_to_all(queries, "ctx", split_axis=1, concat_axis=0, tiled=True),
        lax.all_to_all(keys, "ctx", split_axis=1, concat_axis=0, tiled=True),
        lax.all_to_all(values, "ctx", split_axis=1, concat_axis=0, tiled=True),
    )
    groups = lax.axis_size("ctx")
    attn_heads = attend(head_q, head_k, head_v, HEADS // groups)
    group_rows = lax.all_gather(out_weight, "dp", axis=1, tiled=True)
    summed = lax.psum_scatter(
        jnp.dot(attn_heads, group_rows, preferred_element_type=jnp.float32).astype(jnp.bfloat16),
        "ctx",
        scatter_dimension=0,
        tiled=True,
    )
    attn_float = lax.optimization_barrier(summed).astype(jnp.float32)
    mixed = deepnorm_alpha * residual_in.astype(jnp.float32) + attn_float
    mean = jnp.mean(mixed, axis=-1, keepdims=True)
    centered = mixed - mean
    var = jnp.mean(centered * centered, axis=-1, keepdims=True)
    normed = centered * lax.rsqrt(var + norm_eps) * norm_gain + norm_bias
    return normed.astype(jnp.bfloat16)


MESH = pl.DeviceIdType.MESH


def fused_kernel(
    q_ref, k_ref, v_ref, w_ref, res_ref, gain_ref, bias_ref, out_ref,
    qh, kh, vh, wf_hub, wf_chain, op, op2, ostage,
    upr_hub, dnr_hub, stage_hub, own_hub, pbuf_hub,
    upr_chain, dnr_chain, stage_chain, own_chain, pbuf_chain,
    s_send, s_recv, s_local, w_send, w_recv, w_local,
    o_send, o_recv, o2_send, o2_recv,
    up_send, up_recv, dn_send, dn_recv,
):
    rows = q_ref.shape[0]
    hd = qh.shape[2]
    heads = qh.shape[0]
    group = heads * hd
    columns = w_ref.shape[1]
    chunks = (own_hub.shape[2], own_chain.shape[2])
    starts = (0, chunks[0])
    uprs, dnrs = (upr_hub, upr_chain), (dnr_hub, dnr_chain)
    stages, owns = (stage_hub, stage_chain), (own_hub, own_chain)
    pbufs = (pbuf_hub, pbuf_chain)
    dp = lax.axis_index("dp")
    ctx = lax.axis_index("ctx")
    xi, core = dp // 2, dp % 2
    zi, yi = ctx // 2, ctx % 2
    sib = (xi * 2 + (1 - core), ctx)
    xnb = ((1 - xi) * 2 + core, ctx)
    ynb = (dp, zi * 2 + (1 - yi))
    is_hub = jnp.logical_and(zi >= 1, zi <= 2)
    is_feeder = jnp.logical_or(zi == 0, zi == 3)
    hub = 1 + zi // 2
    feeder = (zi // 2) * 3

    barrier = pltpu.get_barrier_semaphore()
    for d in range(1, 8):
        pl.semaphore_signal(barrier, inc=1, device_id=(dp, (ctx + d) % 8), device_id_type=MESH)
    for peer in (sib, xnb):
        pl.semaphore_signal(barrier, inc=1, device_id=peer, device_id_type=MESH)
    pl.semaphore_wait(barrier, 9)

    sources = (q_ref, k_ref, v_ref)
    landing = (qh, kh, vh)

    def cols_of(target, h):
        return pl.ds(pl.multiple_of(target * group + h * hd, hd), hd)

    def rows_of(block):
        return pl.ds(pl.multiple_of(block * rows, rows), rows)

    def qkv_copy(a, h, target):
        return pltpu.make_async_remote_copy(
            src_ref=sources[a].at[:, cols_of(target, h)],
            dst_ref=landing[a].at[h, rows_of(ctx), :],
            send_sem=s_send.at[a, h, target],
            recv_sem=s_recv.at[a, h, ctx],
            device_id=(dp, target),
            device_id_type=MESH,
        )

    def qkv_arrival(a, h, source):
        place = landing[a].at[h, rows_of(source), :]
        return pltpu.make_async_remote_copy(
            src_ref=place, dst_ref=place,
            send_sem=s_send.at[a, h, source], recv_sem=s_recv.at[a, h, source],
            device_id=(dp, source), device_id_type=MESH,
        )

    def qkv_local(a, h):
        return pltpu.make_async_copy(
            sources[a].at[:, cols_of(ctx, h)], landing[a].at[h, rows_of(ctx), :], s_local.at[a, h]
        )

    def w_place(part, slot_y, slot_d):
        return wf_chain.at[slot_y, slot_d] if part == 1 else wf_hub.at[part // 2, slot_y, slot_d]

    def w_copy(part, slot_y, slot_d, peer, number, first=False):
        place = w_place(part, slot_y, slot_d)
        return pltpu.make_async_remote_copy(
            src_ref=w_ref.at[:, pl.ds(starts[part % 2], chunks[part % 2])] if first else place,
            dst_ref=place,
            send_sem=w_send.at[number, part],
            recv_sem=w_recv.at[part, slot_y, slot_d],
            device_id=peer,
            device_id_type=MESH,
        )

    xdp = xnb[0]
    routes = {
        0: (yi, dp, xnb),
        1: (yi, dp, ynb),
        2: (yi, dp, sib),
        3: (yi, xdp, sib),
        4: (1 - yi, dp, sib),
        5: (1 - yi, dp, xnb),
        6: (1 - yi, xdp, sib),
    }

    def forward(number, part):
        slot_y, slot_d, peer = routes[number]
        return w_copy(part, slot_y, slot_d, peer, number, number < 3 and part < 2)

    def w_arrive(part, slot_y, slot_d):
        w_copy(part, slot_y, slot_d, ynb, 0).wait_recv()

    def feed_w():
        return w_copy(2, yi, dp, (dp, hub * 2 + yi), 7, True)

    def keep_w(part):
        return pltpu.make_async_copy(
            w_ref.at[:, pl.ds(starts[part], chunks[part])], w_place(part, yi, dp), w_local.at[part]
        )

    for h in range(heads):
        for d in (4, 3, 5, 2, 6, 1, 7):
            for a in range(3):
                qkv_copy(a, h, (ctx + d) % 8).start()
        for a in range(3):
            qkv_local(a, h).start()
        if h == 0 or h == 2:
            forward(h, 1).start()

            @pl.when(is_hub)
            def _():
                forward(h, 0).start()

        if h == 0:
            @pl.when(is_feeder)
            def _():
                feed_w().start()

        if h == 1:
            forward(1, 1).start()

    for part in range(2):
        keep_w(part).start()

    factor = math.log2(math.e) / math.sqrt(hd)
    block = 2 * rows

    def o_copy(h):
        return pltpu.make_async_remote_copy(
            src_ref=ostage.at[h],
            dst_ref=op.at[yi, h],
            send_sem=o_send.at[h],
            recv_sem=o_recv.at[h],
            device_id=ynb,
            device_id_type=MESH,
        )

    def feed_o(h, y):
        return pltpu.make_async_remote_copy(
            src_ref=op.at[y, h],
            dst_ref=op2.at[y, h],
            send_sem=o2_send.at[y, h],
            recv_sem=o2_recv.at[y, h],
            device_id=(dp, hub * 2 + yi),
            device_id_type=MESH,
        )

    def other_half(h):
        place = op.at[1 - yi, h]
        pltpu.make_async_remote_copy(
            src_ref=place, dst_ref=place, send_sem=o_send.at[h], recv_sem=o_recv.at[h],
            device_id=ynb, device_id_type=MESH,
        ).wait_recv()

        @pl.when(is_feeder)
        def _():
            feed_o(h, 1 - yi).start()

    def one_head(h, carry):
        def arrived(d, inner):
            for a in range(3):
                qkv_arrival(a, h, (ctx + d) % 8).wait_recv()
            return inner

        lax.fori_loop(1, 8, arrived, 0)
        for a in range(3):
            qkv_local(a, h).wait()
        for t in range(4):
            length = block * (t + 1)
            scores = lax.dot_general(
                qh[h, t * block : length, :], kh[h, :length, :],
                (((1,), (1,)), ((), ())), preferred_element_type=jnp.float32,
            )
            at_row = lax.broadcasted_iota(jnp.int32, (block, block), 0)
            at_col = lax.broadcasted_iota(jnp.int32, (block, block), 1)
            diagonal = jnp.where(at_row >= at_col, scores[:, t * block :], -1e30)
            if t > 0:
                scores = jnp.concatenate([scores[:, : t * block], diagonal], axis=1)
            else:
                scores = diagonal
            highest = jnp.max(scores, axis=-1, keepdims=True)
            expo = jnp.exp2((scores - highest) * factor)
            total = jnp.sum(expo, axis=-1, keepdims=True)
            result = jnp.dot(
                expo.astype(jnp.bfloat16), vh[h, :length, :], preferred_element_type=jnp.float32
            ) / total
            low, high = result[:rows], result[rows:]
            mine = jnp.where(yi == 0, low, high)
            theirs = jnp.where(yi == 0, high, low)
            op[yi, h, t * rows : (t + 1) * rows, :] = mine.astype(jnp.bfloat16)
            ostage[h, t * rows : (t + 1) * rows, :] = theirs.astype(jnp.bfloat16)
        o_copy(h).start()

        @pl.when(is_feeder)
        def _():
            feed_o(h, yi).start()

        @pl.when(h > 0)
        def _():
            other_half(h - 1)

        @pl.when(h == 1)
        def _():
            w_arrive(1, yi, xdp)
            forward(3, 1).start()

            @pl.when(is_hub)
            def _():
                forward(1, 0).start()

        @pl.when(jnp.logical_and(h == 2, is_hub))
        def _():
            w_arrive(2, yi, dp)
            forward(0, 2).start()
            forward(2, 2).start()
            w_arrive(0, yi, xdp)
            forward(3, 0).start()

        return carry

    lax.fori_loop(0, heads, one_head, 0)

    @pl.when(is_hub)
    def _():
        forward(1, 2).start()

    w_arrive(1, 1 - yi, dp)
    forward(5, 1).start()
    forward(4, 1).start()
    other_half(heads - 1)
    for part in range(2):
        keep_w(part).wait()

    def chain_copy(up, t, j, d):
        slot = t - 1 if up else t
        to = jnp.minimum(zi + 1, 3) if up else jnp.maximum(zi - 1, 0)
        return pltpu.make_async_remote_copy(
            src_ref=stages[j].at[slot, d],
            dst_ref=(uprs if up else dnrs)[j].at[slot, d],
            send_sem=(up_send if up else dn_send).at[slot, d * 2 + j],
            recv_sem=(up_recv if up else dn_recv).at[slot, d * 2 + j],
            device_id=(dp, to * 2 + yi),
            device_id_type=MESH,
        )

    def sends_here(up, t, hubs):
        sends = zi < t if up else zi > t
        if hubs:
            sends = jnp.logical_and(sends, zi >= 1 if up else zi <= 2)
        return sends

    def relay(up, t, j, d, allowed):
        hubs = j == 0
        slot = t - 1 if up else t
        there, stage, pbuf = (uprs if up else dnrs)[j], stages[j], pbufs[j]
        sends = jnp.logical_and(allowed, sends_here(up, t, hubs))
        first = (1 if hubs else 0) if up else (2 if hubs else 3)

        @pl.when(jnp.logical_and(sends, zi == first))
        def _():
            stage[slot, d] = pbuf[t].astype(jnp.bfloat16)
            chain_copy(up, t, j, d).start()

        @pl.when(jnp.logical_and(sends, zi != first))
        def _():
            chain_copy(up, t, j, d).wait_recv()
            stage[slot, d] = (pbuf[t] + there[slot, d].astype(jnp.float32)).astype(jnp.bfloat16)
            chain_copy(up, t, j, d).start()

    def relays(j, d):
        hubs = j == 0
        lower, upper = zi < 2, zi >= 2
        ups = (3, 2) if hubs else (3, 2, 1)
        downs = (0, 1) if hubs else (0, 1, 2)
        for t in ups:
            relay(True, t, j, d, lower)
        for t in downs:
            relay(False, t, j, d, upper)
        for t in ups:
            relay(True, t, j, d, upper)
        for t in downs:
            relay(False, t, j, d, lower)

    def owner(i):
        return ((xi + i // 2) % 2) * 2 + (core + i) % 2

    def wait_chain(up, slot, j, d):
        place = (uprs if up else dnrs)[j].at[slot, d]
        at = d * 2 + j
        pltpu.make_async_remote_copy(
            src_ref=place, dst_ref=place, send_sem=(up_send if up else dn_send).at[slot, at],
            recv_sem=(up_recv if up else dn_recv).at[slot, at], device_id=ynb, device_id_type=MESH,
        ).wait_recv()

    def finish(i, total):
        d = owner(i)
        for j in (1, 0):
            own = owns[j]

            @pl.when(zi > (1 if j == 0 else 0))
            def _():
                wait_chain(True, zi - 1, j, d)
                own[d] += uprs[j][zi - 1, d].astype(jnp.float32)

            @pl.when(zi < (2 if j == 0 else 3))
            def _():
                wait_chain(False, zi, j, d)
                own[d] += dnrs[j][zi, d].astype(jnp.float32)

            cols = pl.ds(pl.multiple_of(d * columns + starts[j], 128), chunks[j])
            res = res_ref[:, cols].astype(jnp.float32)
            mixed = deepnorm_alpha * res + own[d].astype(jnp.bfloat16).astype(jnp.float32)
            own[d] = mixed
            total = total + jnp.sum(mixed, axis=-1, keepdims=True)
        return total

    def heads_of(ref):
        return jnp.concatenate([ref[y, h] for y in range(2) for h in range(heads)], axis=1)

    def product(lhs, rhs):
        wide = rhs.shape[-1]
        return jnp.dot(
            lhs, rhs.reshape(2 * group, wide), preferred_element_type=jnp.float32
        ).reshape(4, rows, wide)

    def one_step(i, total):
        @pl.when(i < 4)
        def _():
            d = owner(i)

            @pl.when(i % 2 == 1)
            def _():
                for y in range(2):
                    w_arrive(1, y, d)

            pbuf_chain[...] = product(heads_of(op), wf_chain[:, d])
            relays(1, d)
            own_chain[d] = pbuf_chain[zi]

            @pl.when(i == 1)
            def _():
                w_arrive(1, 1 - yi, xdp)
                forward(6, 1).start()

        @pl.when(jnp.logical_and(i == 0, is_hub))
        def _():
            w_arrive(0, 1 - yi, dp)
            forward(5, 0).start()
            forward(4, 0).start()
            w_arrive(2, yi, xdp)
            forward(3, 2).start()

        @pl.when(jnp.logical_and(i == 1, is_hub))
        def _():
            w_arrive(2, 1 - yi, dp)
            forward(5, 2).start()
            forward(4, 2).start()
            for h in range(heads):
                for y in range(2):
                    place = op2.at[y, h]
                    pltpu.make_async_remote_copy(
                        src_ref=place, dst_ref=place, send_sem=o2_send.at[0, h],
                        recv_sem=o2_recv.at[y, h], device_id=ynb, device_id_type=MESH,
                    ).wait_recv()

        @pl.when(jnp.logical_and(i >= 1, is_hub))
        def _():
            d = owner(i - 1)

            @pl.when(i % 2 == 0)
            def _():
                for y in range(2):
                    w_arrive(0, y, d)
                    w_arrive(2, y, d)

            pbuf_hub[...] = product(heads_of(op), wf_hub[0, :, d])
            pbuf_hub[...] += product(heads_of(op2), wf_hub[1, :, d])
            relays(0, d)
            own_hub[d] = pbuf_hub[zi]

            @pl.when(i == 2)
            def _():
                for part in (0, 2):
                    w_arrive(part, 1 - yi, xdp)
                    forward(6, part).start()

        @pl.when(jnp.logical_and(i >= 1, is_feeder))
        def _():
            own_hub[owner(i - 1)] = jnp.zeros(own_hub.shape[1:], jnp.float32)

        return lax.cond(i > 2, lambda: finish(i - 3, total), lambda: total)

    total = lax.fori_loop(0, 5, one_step, jnp.zeros((rows, 1), jnp.float32))
    total = finish(2, total)
    total = finish(3, total)

    width = columns * 4
    mean = total / width
    squares = jnp.zeros((rows, 1), jnp.float32)
    for own in owns:
        for d in range(4):
            centered = own[d] - mean
            squares += jnp.sum(centered * centered, axis=-1, keepdims=True)
    inverse = lax.rsqrt(squares / width + norm_eps)
    for j, own in enumerate(owns):
        for d in range(4):
            low = d * columns + starts[j]
            cols = slice(low, low + chunks[j])
            normed = (own[d] - mean) * inverse * gain_ref[:, cols] + bias_ref[:, cols]
            out_ref[:, cols] = normed.astype(out_ref.dtype)

    def sent_qkv(h, carry):
        def sent(d, inner):
            for a in range(3):
                qkv_copy(a, h, (ctx + d) % 8).wait_send()
            return inner

        lax.fori_loop(1, 8, sent, 0)
        o_copy(h).wait_send()

        @pl.when(is_feeder)
        def _():
            feed_o(h, 0).wait_send()
            feed_o(h, 1).wait_send()

        return carry

    lax.fori_loop(0, heads, sent_qkv, 0)
    for number in routes:
        forward(number, 1).wait_send()

    @pl.when(is_feeder)
    def _():
        feed_w().wait_send()

    @pl.when(is_hub)
    def _():
        for number in routes:
            for part in (0, 2):
                forward(number, part).wait_send()

    def sent_chain(d, carry):
        for j in range(2):
            for up, targets in ((True, (3, 2, 1)), (False, (0, 1, 2))):
                for t in targets:
                    @pl.when(sends_here(up, t, j == 0))
                    def _():
                        chain_copy(up, t, j, d).wait_send()
        return carry

    lax.fori_loop(0, 4, sent_chain, 0)


def local_fused(queries, keys, values, residual_in, out_weight, norm_gain, norm_bias):
    rows, width = residual_in.shape
    group, columns = out_weight.shape
    hd = queries.shape[1] // HEADS
    heads = group // hd
    length = rows * 8
    hub_part = columns // 7 * 4
    chain_part = columns - hub_part
    bf16, f32 = jnp.bfloat16, jnp.float32
    dma = pltpu.SemaphoreType.DMA
    in_vmem = pl.BlockSpec(memory_space=pltpu.VMEM)
    in_any = pl.BlockSpec(memory_space=pl.ANY)
    return pl.pallas_call(
        fused_kernel,
        out_shape=jax.ShapeDtypeStruct((rows, width), bf16),
        in_specs=[in_any] * 4 + [in_vmem] * 3,
        out_specs=in_vmem,
        scratch_shapes=[
            pltpu.VMEM((heads, length, hd), bf16),
            pltpu.VMEM((heads, length, hd), bf16),
            pltpu.VMEM((heads, length, hd), bf16),
            pltpu.VMEM((2, 2, 4, group, hub_part), bf16),
            pltpu.VMEM((2, 4, group, chain_part), bf16),
            pltpu.VMEM((2, heads, length // 2, hd), bf16),
            pltpu.VMEM((2, heads, length // 2, hd), bf16),
            pltpu.VMEM((heads, length // 2, hd), bf16),
        ] + [
            pltpu.VMEM(shape + (rows, part), kind)
            for part in (hub_part, chain_part)
            for shape, kind in (((3, 4), bf16),) * 3 + (((4,), f32),) * 2
        ] + [
            dma((3, heads, 8)), dma((3, heads, 8)), dma((3, heads)),
            dma((8, 3)), dma((3, 2, 4)), dma((2,)),
            dma((heads,)), dma((heads,)), dma((2, heads)), dma((2, heads)),
            dma((3, 8)), dma((3, 8)), dma((3, 8)), dma((3, 8)),
        ],
        compiler_params=pltpu.CompilerParams(
            collective_id=0, has_side_effects=True, vmem_limit_bytes=60 * 1024 * 1024
        ),
    )(
        queries, keys, values, out_weight, residual_in,
        norm_gain.reshape(1, width), norm_bias.reshape(1, width),
    )


def solution(mesh):
    in_specs = (
        P(("dp", "ctx"), None),
        P(("dp", "ctx"), None),
        P(("dp", "ctx"), None),
        P(("dp", "ctx"), None),
        P("ctx", "dp"),
        P(),
        P(),
    )
    out_specs = P(("dp", "ctx"), None)
    fused = mesh.shape["dp"] == 4 and mesh.shape["ctx"] == 8
    local = local_fused if fused else local_general
    return jax.shard_map(local, mesh=mesh, in_specs=in_specs, out_specs=out_specs, check_vma=False)
```

```python
import math

import jax
import jax.numpy as jnp
from jax import lax
from jax.experimental import pallas as pl
from jax.experimental.pallas import tpu as pltpu
from jax.sharding import PartitionSpec as P

HEADS = 32


deepnorm_alpha = 96.0**0.25
norm_eps = 1e-05


def block_rows(length):
    block = min(512, length)
    while length % block != 0:
        block = block + 1
    return block


def attend(all_queries, all_keys, all_values, local_heads):
    length = all_queries.shape[0]
    width = all_queries.shape[1]
    head_dim = width // local_heads
    block = block_rows(length)
    blocks = length // block
    scale = 1.0 / math.sqrt(head_dim)
    query_blocks = all_queries.reshape(blocks, block, local_heads, head_dim)
    key_heads = all_keys.reshape(length, local_heads, head_dim)
    value_heads = all_values.reshape(length, local_heads, head_dim)
    key_position = jnp.arange(length)

    def one_block(inputs):
        number, query_part = inputs
        scores = (
            jnp.einsum("qhd,khd->hqk", query_part, key_heads, preferred_element_type=jnp.float32)
            * scale
        )
        query_position = number * block + jnp.arange(block)
        causal = query_position[:, None] >= key_position[None, :]
        scores = jnp.where(causal[None], scores, -1e30)
        highest = jnp.max(scores, axis=-1, keepdims=True)
        expo = jnp.exp(scores - highest)
        probs = (expo / jnp.sum(expo, axis=-1, keepdims=True)).astype(jnp.bfloat16)
        result = jnp.einsum("hqk,khd->qhd", probs, value_heads, preferred_element_type=jnp.float32)
        return result.astype(jnp.bfloat16).reshape(block, width)

    outputs = lax.map(one_block, (jnp.arange(blocks), query_blocks))
    return outputs.reshape(length, width)


def local_general(queries, keys, values, residual_in, out_weight, norm_gain, norm_bias):
    head_q, head_k, head_v = (
        lax.all_to_all(queries, "ctx", split_axis=1, concat_axis=0, tiled=True),
        lax.all_to_all(keys, "ctx", split_axis=1, concat_axis=0, tiled=True),
        lax.all_to_all(values, "ctx", split_axis=1, concat_axis=0, tiled=True),
    )
    groups = lax.axis_size("ctx")
    attn_heads = attend(head_q, head_k, head_v, HEADS // groups)
    group_rows = lax.all_gather(out_weight, "dp", axis=1, tiled=True)
    summed = lax.psum_scatter(
        jnp.dot(attn_heads, group_rows, preferred_element_type=jnp.float32).astype(jnp.bfloat16),
        "ctx",
        scatter_dimension=0,
        tiled=True,
    )
    attn_float = lax.optimization_barrier(summed).astype(jnp.float32)
    mixed = deepnorm_alpha * residual_in.astype(jnp.float32) + attn_float
    mean = jnp.mean(mixed, axis=-1, keepdims=True)
    centered = mixed - mean
    var = jnp.mean(centered * centered, axis=-1, keepdims=True)
    normed = centered * lax.rsqrt(var + norm_eps) * norm_gain + norm_bias
    return normed.astype(jnp.bfloat16)


MESH = pl.DeviceIdType.MESH


def fused_kernel(
    q_ref, k_ref, v_ref, w_ref, res_ref, gain_ref, bias_ref, out_ref,
    qh, kh, vh, wf_hub, wf_chain, op, op2, ostage,
    upr_hub, dnr_hub, stage_hub, own_hub, pbuf_hub,
    upr_chain, dnr_chain, stage_chain, own_chain, pbuf_chain,
    s_send, s_recv, s_local, w_send, w_recv, w_local,
    o_send, o_recv, o2_send, o2_recv,
    up_send, up_recv, dn_send, dn_recv,
):
    rows = q_ref.shape[0]
    hd = qh.shape[2]
    heads = qh.shape[0]
    group = heads * hd
    columns = w_ref.shape[1]
    chunks = (own_hub.shape[2], own_chain.shape[2])
    starts = (0, chunks[0])
    uprs, dnrs = (upr_hub, upr_chain), (dnr_hub, dnr_chain)
    stages, owns = (stage_hub, stage_chain), (own_hub, own_chain)
    pbufs = (pbuf_hub, pbuf_chain)
    dp = lax.axis_index("dp")
    ctx = lax.axis_index("ctx")
    xi, core = dp // 2, dp % 2
    zi, yi = ctx // 2, ctx % 2
    sib = (xi * 2 + (1 - core), ctx)
    xnb = ((1 - xi) * 2 + core, ctx)
    ynb = (dp, zi * 2 + (1 - yi))
    is_hub = jnp.logical_and(zi >= 1, zi <= 2)
    is_feeder = jnp.logical_or(zi == 0, zi == 3)
    hub = 1 + zi // 2
    feeder = (zi // 2) * 3

    barrier = pltpu.get_barrier_semaphore()
    for d in range(1, 8):
        pl.semaphore_signal(barrier, inc=1, device_id=(dp, (ctx + d) % 8), device_id_type=MESH)
    for peer in (sib, xnb):
        pl.semaphore_signal(barrier, inc=1, device_id=peer, device_id_type=MESH)
    pl.semaphore_wait(barrier, 9)

    sources = (q_ref, k_ref, v_ref)
    landing = (qh, kh, vh)

    def cols_of(target, h):
        return pl.ds(pl.multiple_of(target * group + h * hd, hd), hd)

    def rows_of(block):
        return pl.ds(pl.multiple_of(block * rows, rows), rows)

    def qkv_copy(a, h, target):
        return pltpu.make_async_remote_copy(
            src_ref=sources[a].at[:, cols_of(target, h)],
            dst_ref=landing[a].at[h, rows_of(ctx), :],
            send_sem=s_send.at[a, h, target],
            recv_sem=s_recv.at[a, h, ctx],
            device_id=(dp, target),
            device_id_type=MESH,
        )

    def qkv_arrival(a, h, source):
        place = landing[a].at[h, rows_of(source), :]
        return pltpu.make_async_remote_copy(
            src_ref=place, dst_ref=place,
            send_sem=s_send.at[a, h, source], recv_sem=s_recv.at[a, h, source],
            device_id=(dp, source), device_id_type=MESH,
        )

    def qkv_local(a, h):
        return pltpu.make_async_copy(
            sources[a].at[:, cols_of(ctx, h)], landing[a].at[h, rows_of(ctx), :], s_local.at[a, h]
        )

    def w_place(part, slot_y, slot_d):
        return wf_chain.at[slot_y, slot_d] if part == 1 else wf_hub.at[part // 2, slot_y, slot_d]

    def w_copy(part, slot_y, slot_d, peer, number, first=False):
        place = w_place(part, slot_y, slot_d)
        return pltpu.make_async_remote_copy(
            src_ref=w_ref.at[:, pl.ds(starts[part % 2], chunks[part % 2])] if first else place,
            dst_ref=place,
            send_sem=w_send.at[number, part],
            recv_sem=w_recv.at[part, slot_y, slot_d],
            device_id=peer,
            device_id_type=MESH,
        )

    xdp = xnb[0]
    routes = {
        0: (yi, dp, xnb),
        1: (yi, dp, ynb),
        2: (yi, dp, sib),
        3: (yi, xdp, sib),
        4: (1 - yi, dp, sib),
        5: (1 - yi, dp, xnb),
        6: (1 - yi, xdp, sib),
    }

    def forward(number, part):
        slot_y, slot_d, peer = routes[number]
        return w_copy(part, slot_y, slot_d, peer, number, number < 3 and part < 2)

    def w_arrive(part, slot_y, slot_d):
        w_copy(part, slot_y, slot_d, ynb, 0).wait_recv()

    def feed_w():
        return w_copy(2, yi, dp, (dp, hub * 2 + yi), 7, True)

    def keep_w(part):
        return pltpu.make_async_copy(
            w_ref.at[:, pl.ds(starts[part], chunks[part])], w_place(part, yi, dp), w_local.at[part]
        )

    for h in range(heads):
        for d in (4, 3, 5, 2, 6, 1, 7):
            for a in range(3):
                qkv_copy(a, h, (ctx + d) % 8).start()
        for a in range(3):
            qkv_local(a, h).start()
        if h == 0 or h == 2:
            forward(h, 1).start()

            @pl.when(is_hub)
            def _():
                forward(h, 0).start()

        if h == 0:
            @pl.when(is_feeder)
            def _():
                feed_w().start()

        if h == 1:
            forward(1, 1).start()

    for part in range(2):
        keep_w(part).start()

    factor = math.log2(math.e) / math.sqrt(hd)
    block = 2 * rows

    def o_copy(h):
        return pltpu.make_async_remote_copy(
            src_ref=ostage.at[h],
            dst_ref=op.at[yi, h],
            send_sem=o_send.at[h],
            recv_sem=o_recv.at[h],
            device_id=ynb,
            device_id_type=MESH,
        )

    def feed_o(h, y):
        return pltpu.make_async_remote_copy(
            src_ref=op.at[y, h],
            dst_ref=op2.at[y, h],
            send_sem=o2_send.at[y, h],
            recv_sem=o2_recv.at[y, h],
            device_id=(dp, hub * 2 + yi),
            device_id_type=MESH,
        )

    def other_half(h):
        place = op.at[1 - yi, h]
        pltpu.make_async_remote_copy(
            src_ref=place, dst_ref=place, send_sem=o_send.at[h], recv_sem=o_recv.at[h],
            device_id=ynb, device_id_type=MESH,
        ).wait_recv()

        @pl.when(is_feeder)
        def _():
            feed_o(h, 1 - yi).start()

    def one_head(h, carry):
        def arrived(d, inner):
            for a in range(3):
                qkv_arrival(a, h, (ctx + d) % 8).wait_recv()
            return inner

        lax.fori_loop(1, 8, arrived, 0)
        for a in range(3):
            qkv_local(a, h).wait()
        for t in range(4):
            length = block * (t + 1)
            scores = lax.dot_general(
                qh[h, t * block : length, :], kh[h, :length, :],
                (((1,), (1,)), ((), ())), preferred_element_type=jnp.float32,
            )
            at_row = lax.broadcasted_iota(jnp.int32, (block, block), 0)
            at_col = lax.broadcasted_iota(jnp.int32, (block, block), 1)
            diagonal = jnp.where(at_row >= at_col, scores[:, t * block :], -1e30)
            if t > 0:
                scores = jnp.concatenate([scores[:, : t * block], diagonal], axis=1)
            else:
                scores = diagonal
            highest = jnp.max(scores, axis=-1, keepdims=True)
            expo = jnp.exp2((scores - highest) * factor)
            total = jnp.sum(expo, axis=-1, keepdims=True)
            result = jnp.dot(
                expo.astype(jnp.bfloat16), vh[h, :length, :], preferred_element_type=jnp.float32
            ) / total
            low, high = result[:rows], result[rows:]
            mine = jnp.where(yi == 0, low, high)
            theirs = jnp.where(yi == 0, high, low)
            op[yi, h, t * rows : (t + 1) * rows, :] = mine.astype(jnp.bfloat16)
            ostage[h, t * rows : (t + 1) * rows, :] = theirs.astype(jnp.bfloat16)
        o_copy(h).start()

        @pl.when(is_feeder)
        def _():
            feed_o(h, yi).start()

        @pl.when(h > 0)
        def _():
            other_half(h - 1)

        @pl.when(h == 1)
        def _():
            w_arrive(1, yi, xdp)
            forward(3, 1).start()

            @pl.when(is_hub)
            def _():
                forward(1, 0).start()

        @pl.when(jnp.logical_and(h == 2, is_hub))
        def _():
            w_arrive(2, yi, dp)
            forward(0, 2).start()
            forward(2, 2).start()
            w_arrive(0, yi, xdp)
            forward(3, 0).start()

        return carry

    lax.fori_loop(0, heads, one_head, 0)

    @pl.when(is_hub)
    def _():
        forward(1, 2).start()

    w_arrive(1, 1 - yi, dp)
    forward(5, 1).start()
    forward(4, 1).start()
    other_half(heads - 1)
    for part in range(2):
        keep_w(part).wait()

    def chain_copy(up, t, j, d):
        slot = t - 1 if up else t
        to = jnp.minimum(zi + 1, 3) if up else jnp.maximum(zi - 1, 0)
        return pltpu.make_async_remote_copy(
            src_ref=stages[j].at[slot, d],
            dst_ref=(uprs if up else dnrs)[j].at[slot, d],
            send_sem=(up_send if up else dn_send).at[slot, d * 2 + j],
            recv_sem=(up_recv if up else dn_recv).at[slot, d * 2 + j],
            device_id=(dp, to * 2 + yi),
            device_id_type=MESH,
        )

    def sends_here(up, t, hubs):
        sends = zi < t if up else zi > t
        if hubs:
            sends = jnp.logical_and(sends, zi >= 1 if up else zi <= 2)
        return sends

    def relay(up, t, j, d, allowed):
        hubs = j == 0
        slot = t - 1 if up else t
        there, stage, pbuf = (uprs if up else dnrs)[j], stages[j], pbufs[j]
        sends = jnp.logical_and(allowed, sends_here(up, t, hubs))
        first = (1 if hubs else 0) if up else (2 if hubs else 3)

        @pl.when(jnp.logical_and(sends, zi == first))
        def _():
            stage[slot, d] = pbuf[t].astype(jnp.bfloat16)
            chain_copy(up, t, j, d).start()

        @pl.when(jnp.logical_and(sends, zi != first))
        def _():
            chain_copy(up, t, j, d).wait_recv()
            stage[slot, d] = (pbuf[t] + there[slot, d].astype(jnp.float32)).astype(jnp.bfloat16)
            chain_copy(up, t, j, d).start()

    def relays(j, d):
        hubs = j == 0
        lower, upper = zi < 2, zi >= 2
        ups = (3, 2) if hubs else (3, 2, 1)
        downs = (0, 1) if hubs else (0, 1, 2)
        for t in ups:
            relay(True, t, j, d, lower)
        for t in downs:
            relay(False, t, j, d, upper)
        for t in ups:
            relay(True, t, j, d, upper)
        for t in downs:
            relay(False, t, j, d, lower)

    def owner(i):
        return ((xi + i // 2) % 2) * 2 + (core + i) % 2

    def wait_chain(up, slot, j, d):
        place = (uprs if up else dnrs)[j].at[slot, d]
        at = d * 2 + j
        pltpu.make_async_remote_copy(
            src_ref=place, dst_ref=place, send_sem=(up_send if up else dn_send).at[slot, at],
            recv_sem=(up_recv if up else dn_recv).at[slot, at], device_id=ynb, device_id_type=MESH,
        ).wait_recv()

    def finish(i, total):
        d = owner(i)
        for j in (1, 0):
            own = owns[j]

            @pl.when(zi > (1 if j == 0 else 0))
            def _():
                wait_chain(True, zi - 1, j, d)
                own[d] += uprs[j][zi - 1, d].astype(jnp.float32)

            @pl.when(zi < (2 if j == 0 else 3))
            def _():
                wait_chain(False, zi, j, d)
                own[d] += dnrs[j][zi, d].astype(jnp.float32)

            cols = pl.ds(pl.multiple_of(d * columns + starts[j], 128), chunks[j])
            res = res_ref[:, cols].astype(jnp.float32)
            mixed = deepnorm_alpha * res + own[d].astype(jnp.bfloat16).astype(jnp.float32)
            own[d] = mixed
            total = total + jnp.sum(mixed, axis=-1, keepdims=True)
        return total

    def heads_of(ref):
        return jnp.concatenate([ref[y, h] for y in range(2) for h in range(heads)], axis=1)

    def product(lhs, rhs):
        wide = rhs.shape[-1]
        return jnp.dot(
            lhs, rhs.reshape(2 * group, wide), preferred_element_type=jnp.float32
        ).reshape(4, rows, wide)

    def one_step(i, total):
        @pl.when(i < 4)
        def _():
            d = owner(i)

            @pl.when(i % 2 == 1)
            def _():
                for y in range(2):
                    w_arrive(1, y, d)

            pbuf_chain[...] = product(heads_of(op), wf_chain[:, d])
            relays(1, d)
            own_chain[d] = pbuf_chain[zi]

            @pl.when(i == 1)
            def _():
                w_arrive(1, 1 - yi, xdp)
                forward(6, 1).start()

        @pl.when(jnp.logical_and(i == 0, is_hub))
        def _():
            w_arrive(0, 1 - yi, dp)
            forward(5, 0).start()
            forward(4, 0).start()
            w_arrive(2, yi, xdp)
            forward(3, 2).start()

        @pl.when(jnp.logical_and(i == 1, is_hub))
        def _():
            w_arrive(2, 1 - yi, dp)
            forward(5, 2).start()
            forward(4, 2).start()
            for h in range(heads):
                for y in range(2):
                    place = op2.at[y, h]
                    pltpu.make_async_remote_copy(
                        src_ref=place, dst_ref=place, send_sem=o2_send.at[0, h],
                        recv_sem=o2_recv.at[y, h], device_id=ynb, device_id_type=MESH,
                    ).wait_recv()

        @pl.when(jnp.logical_and(i >= 1, is_hub))
        def _():
            d = owner(i - 1)

            @pl.when(i % 2 == 0)
            def _():
                for y in range(2):
                    w_arrive(0, y, d)
                    w_arrive(2, y, d)

            pbuf_hub[...] = product(heads_of(op), wf_hub[0, :, d])
            pbuf_hub[...] += product(heads_of(op2), wf_hub[1, :, d])
            relays(0, d)
            own_hub[d] = pbuf_hub[zi]

            @pl.when(i == 2)
            def _():
                for part in (0, 2):
                    w_arrive(part, 1 - yi, xdp)
                    forward(6, part).start()

        @pl.when(jnp.logical_and(i >= 1, is_feeder))
        def _():
            own_hub[owner(i - 1)] = jnp.zeros(own_hub.shape[1:], jnp.float32)

        return lax.cond(i > 2, lambda: finish(i - 3, total), lambda: total)

    total = lax.fori_loop(0, 5, one_step, jnp.zeros((rows, 1), jnp.float32))
    total = finish(2, total)
    total = finish(3, total)

    width = columns * 4
    mean = total / width
    squares = jnp.zeros((rows, 1), jnp.float32)
    for own in owns:
        for d in range(4):
            centered = own[d] - mean
            squares += jnp.sum(centered * centered, axis=-1, keepdims=True)
    inverse = lax.rsqrt(squares / width + norm_eps)
    for j, own in enumerate(owns):
        for d in range(4):
            low = d * columns + starts[j]
            cols = slice(low, low + chunks[j])
            normed = (own[d] - mean) * inverse * gain_ref[:, cols] + bias_ref[:, cols]
            out_ref[:, cols] = normed.astype(out_ref.dtype)

    def sent_qkv(h, carry):
        def sent(d, inner):
            for a in range(3):
                qkv_copy(a, h, (ctx + d) % 8).wait_send()
            return inner

        lax.fori_loop(1, 8, sent, 0)
        o_copy(h).wait_send()

        @pl.when(is_feeder)
        def _():
            feed_o(h, 0).wait_send()
            feed_o(h, 1).wait_send()

        return carry

    lax.fori_loop(0, heads, sent_qkv, 0)
    for number in routes:
        forward(number, 1).wait_send()

    @pl.when(is_feeder)
    def _():
        feed_w().wait_send()

    @pl.when(is_hub)
    def _():
        for number in routes:
            for part in (0, 2):
                forward(number, part).wait_send()

    def sent_chain(d, carry):
        for j in range(2):
            for up, targets in ((True, (3, 2, 1)), (False, (0, 1, 2))):
                for t in targets:
                    @pl.when(sends_here(up, t, j == 0))
                    def _():
                        chain_copy(up, t, j, d).wait_send()
        return carry

    lax.fori_loop(0, 4, sent_chain, 0)


def local_fused(queries, keys, values, residual_in, out_weight, norm_gain, norm_bias):
    rows, width = residual_in.shape
    group, columns = out_weight.shape
    hd = queries.shape[1] // HEADS
    heads = group // hd
    length = rows * 8
    hub_part = columns // 7 * 3
    chain_part = columns - hub_part
    bf16, f32 = jnp.bfloat16, jnp.float32
    dma = pltpu.SemaphoreType.DMA
    in_vmem = pl.BlockSpec(memory_space=pltpu.VMEM)
    in_any = pl.BlockSpec(memory_space=pl.ANY)
    return pl.pallas_call(
        fused_kernel,
        out_shape=jax.ShapeDtypeStruct((rows, width), bf16),
        in_specs=[in_any] * 4 + [in_vmem] * 3,
        out_specs=in_vmem,
        scratch_shapes=[
            pltpu.VMEM((heads, length, hd), bf16),
            pltpu.VMEM((heads, length, hd), bf16),
            pltpu.VMEM((heads, length, hd), bf16),
            pltpu.VMEM((2, 2, 4, group, hub_part), bf16),
            pltpu.VMEM((2, 4, group, chain_part), bf16),
            pltpu.VMEM((2, heads, length // 2, hd), bf16),
            pltpu.VMEM((2, heads, length // 2, hd), bf16),
            pltpu.VMEM((heads, length // 2, hd), bf16),
        ] + [
            pltpu.VMEM(shape + (rows, part), kind)
            for part in (hub_part, chain_part)
            for shape, kind in (((3, 4), bf16),) * 3 + (((4,), f32),) * 2
        ] + [
            dma((3, heads, 8)), dma((3, heads, 8)), dma((3, heads)),
            dma((8, 3)), dma((3, 2, 4)), dma((2,)),
            dma((heads,)), dma((heads,)), dma((2, heads)), dma((2, heads)),
            dma((3, 8)), dma((3, 8)), dma((3, 8)), dma((3, 8)),
        ],
        compiler_params=pltpu.CompilerParams(
            collective_id=0, has_side_effects=True, vmem_limit_bytes=60 * 1024 * 1024
        ),
    )(
        queries, keys, values, out_weight, residual_in,
        norm_gain.reshape(1, width), norm_bias.reshape(1, width),
    )


def solution(mesh):
    in_specs = (
        P(("dp", "ctx"), None),
        P(("dp", "ctx"), None),
        P(("dp", "ctx"), None),
        P(("dp", "ctx"), None),
        P("ctx", "dp"),
        P(),
        P(),
    )
    out_specs = P(("dp", "ctx"), None)
    fused = mesh.shape["dp"] == 4 and mesh.shape["ctx"] == 8
    local = local_fused if fused else local_general
    return jax.shard_map(local, mesh=mesh, in_specs=in_specs, out_specs=out_specs, check_vma=False)
```

```python
import math

import jax
import jax.numpy as jnp
from jax import lax
from jax.experimental import pallas as pl
from jax.experimental.pallas import tpu as pltpu
from jax.sharding import PartitionSpec as P

HEADS = 32


deepnorm_alpha = 96.0**0.25
norm_eps = 1e-05


def block_rows(length):
    block = min(512, length)
    while length % block != 0:
        block = block + 1
    return block


def attend(all_queries, all_keys, all_values, local_heads):
    length = all_queries.shape[0]
    width = all_queries.shape[1]
    head_dim = width // local_heads
    block = block_rows(length)
    blocks = length // block
    scale = 1.0 / math.sqrt(head_dim)
    query_blocks = all_queries.reshape(blocks, block, local_heads, head_dim)
    key_heads = all_keys.reshape(length, local_heads, head_dim)
    value_heads = all_values.reshape(length, local_heads, head_dim)
    key_position = jnp.arange(length)

    def one_block(inputs):
        number, query_part = inputs
        scores = (
            jnp.einsum("qhd,khd->hqk", query_part, key_heads, preferred_element_type=jnp.float32)
            * scale
        )
        query_position = number * block + jnp.arange(block)
        causal = query_position[:, None] >= key_position[None, :]
        scores = jnp.where(causal[None], scores, -1e30)
        highest = jnp.max(scores, axis=-1, keepdims=True)
        expo = jnp.exp(scores - highest)
        probs = (expo / jnp.sum(expo, axis=-1, keepdims=True)).astype(jnp.bfloat16)
        result = jnp.einsum("hqk,khd->qhd", probs, value_heads, preferred_element_type=jnp.float32)
        return result.astype(jnp.bfloat16).reshape(block, width)

    outputs = lax.map(one_block, (jnp.arange(blocks), query_blocks))
    return outputs.reshape(length, width)


def local_general(queries, keys, values, residual_in, out_weight, norm_gain, norm_bias):
    head_q, head_k, head_v = (
        lax.all_to_all(queries, "ctx", split_axis=1, concat_axis=0, tiled=True),
        lax.all_to_all(keys, "ctx", split_axis=1, concat_axis=0, tiled=True),
        lax.all_to_all(values, "ctx", split_axis=1, concat_axis=0, tiled=True),
    )
    groups = lax.axis_size("ctx")
    attn_heads = attend(head_q, head_k, head_v, HEADS // groups)
    group_rows = lax.all_gather(out_weight, "dp", axis=1, tiled=True)
    summed = lax.psum_scatter(
        jnp.dot(attn_heads, group_rows, preferred_element_type=jnp.float32).astype(jnp.bfloat16),
        "ctx",
        scatter_dimension=0,
        tiled=True,
    )
    attn_float = lax.optimization_barrier(summed).astype(jnp.float32)
    mixed = deepnorm_alpha * residual_in.astype(jnp.float32) + attn_float
    mean = jnp.mean(mixed, axis=-1, keepdims=True)
    centered = mixed - mean
    var = jnp.mean(centered * centered, axis=-1, keepdims=True)
    normed = centered * lax.rsqrt(var + norm_eps) * norm_gain + norm_bias
    return normed.astype(jnp.bfloat16)


MESH = pl.DeviceIdType.MESH


def fused_kernel(
    q_ref, k_ref, v_ref, w_ref, res_ref, gain_ref, bias_ref, out_ref,
    qh, kh, vh, wf_hub, wf_chain, op, op2, ostage,
    upr_hub, dnr_hub, stage_hub, own_hub, pbuf_hub,
    upr_chain, dnr_chain, stage_chain, own_chain, pbuf_chain,
    s_send, s_recv, s_local, w_send, w_recv, w_local,
    o_send, o_recv, o2_send, o2_recv,
    up_send, up_recv, dn_send, dn_recv,
):
    rows = q_ref.shape[0]
    hd = qh.shape[2]
    heads = qh.shape[0]
    group = heads * hd
    columns = w_ref.shape[1]
    chunks = (own_hub.shape[2], own_chain.shape[2])
    starts = (0, chunks[0])
    uprs, dnrs = (upr_hub, upr_chain), (dnr_hub, dnr_chain)
    stages, owns = (stage_hub, stage_chain), (own_hub, own_chain)
    pbufs = (pbuf_hub, pbuf_chain)
    dp = lax.axis_index("dp")
    ctx = lax.axis_index("ctx")
    xi, core = dp // 2, dp % 2
    zi, yi = ctx // 2, ctx % 2
    sib = (xi * 2 + (1 - core), ctx)
    xnb = ((1 - xi) * 2 + core, ctx)
    ynb = (dp, zi * 2 + (1 - yi))
    is_hub = jnp.logical_and(zi >= 1, zi <= 2)
    is_feeder = jnp.logical_or(zi == 0, zi == 3)
    hub = 1 + zi // 2
    feeder = (zi // 2) * 3

    barrier = pltpu.get_barrier_semaphore()
    for d in range(1, 8):
        pl.semaphore_signal(barrier, inc=1, device_id=(dp, (ctx + d) % 8), device_id_type=MESH)
    for peer in (sib, xnb):
        pl.semaphore_signal(barrier, inc=1, device_id=peer, device_id_type=MESH)
    pl.semaphore_wait(barrier, 9)

    sources = (q_ref, k_ref, v_ref)
    landing = (qh, kh, vh)

    def cols_of(target, h):
        return pl.ds(pl.multiple_of(target * group + h * hd, hd), hd)

    def rows_of(block):
        return pl.ds(pl.multiple_of(block * rows, rows), rows)

    def qkv_copy(a, h, target):
        return pltpu.make_async_remote_copy(
            src_ref=sources[a].at[:, cols_of(target, h)],
            dst_ref=landing[a].at[h, rows_of(ctx), :],
            send_sem=s_send.at[a, h, target],
            recv_sem=s_recv.at[a, h, ctx],
            device_id=(dp, target),
            device_id_type=MESH,
        )

    def qkv_arrival(a, h, source):
        place = landing[a].at[h, rows_of(source), :]
        return pltpu.make_async_remote_copy(
            src_ref=place, dst_ref=place,
            send_sem=s_send.at[a, h, source], recv_sem=s_recv.at[a, h, source],
            device_id=(dp, source), device_id_type=MESH,
        )

    def qkv_local(a, h):
        return pltpu.make_async_copy(
            sources[a].at[:, cols_of(ctx, h)], landing[a].at[h, rows_of(ctx), :], s_local.at[a, h]
        )

    def w_place(part, slot_y, slot_d):
        return wf_chain.at[slot_y, slot_d] if part == 1 else wf_hub.at[part // 2, slot_y, slot_d]

    def w_copy(part, slot_y, slot_d, peer, number, first=False):
        place = w_place(part, slot_y, slot_d)
        return pltpu.make_async_remote_copy(
            src_ref=w_ref.at[:, pl.ds(starts[part % 2], chunks[part % 2])] if first else place,
            dst_ref=place,
            send_sem=w_send.at[number, part],
            recv_sem=w_recv.at[part, slot_y, slot_d],
            device_id=peer,
            device_id_type=MESH,
        )

    xdp = xnb[0]
    routes = {
        0: (yi, dp, xnb),
        1: (yi, dp, ynb),
        2: (yi, dp, sib),
        3: (yi, xdp, sib),
        4: (1 - yi, dp, sib),
        5: (1 - yi, dp, xnb),
        6: (1 - yi, xdp, sib),
    }

    def forward(number, part):
        slot_y, slot_d, peer = routes[number]
        return w_copy(part, slot_y, slot_d, peer, number, number < 3 and part < 2)

    def w_arrive(part, slot_y, slot_d):
        w_copy(part, slot_y, slot_d, ynb, 0).wait_recv()

    def feed_w():
        return w_copy(2, yi, dp, (dp, hub * 2 + yi), 7, True)

    def keep_w(part):
        return pltpu.make_async_copy(
            w_ref.at[:, pl.ds(starts[part], chunks[part])], w_place(part, yi, dp), w_local.at[part]
        )

    for h in range(heads):
        for d in (4, 3, 5, 2, 6, 1, 7):
            for a in range(3):
                qkv_copy(a, h, (ctx + d) % 8).start()
        for a in range(3):
            qkv_local(a, h).start()
        if h == 0 or h == 2:
            forward(h, 1).start()

            @pl.when(is_hub)
            def _():
                forward(h, 0).start()

        if h == 0:
            @pl.when(is_feeder)
            def _():
                feed_w().start()

        if h == 1:
            forward(1, 1).start()

    for part in range(2):
        keep_w(part).start()

    factor = math.log2(math.e) / math.sqrt(hd)
    block = 2 * rows

    def o_copy(h):
        return pltpu.make_async_remote_copy(
            src_ref=ostage.at[h],
            dst_ref=op.at[yi, h],
            send_sem=o_send.at[h],
            recv_sem=o_recv.at[h],
            device_id=ynb,
            device_id_type=MESH,
        )

    def feed_o(h, y):
        return pltpu.make_async_remote_copy(
            src_ref=op.at[y, h],
            dst_ref=op2.at[y, h],
            send_sem=o2_send.at[y, h],
            recv_sem=o2_recv.at[y, h],
            device_id=(dp, hub * 2 + yi),
            device_id_type=MESH,
        )

    def other_half(h):
        place = op.at[1 - yi, h]
        pltpu.make_async_remote_copy(
            src_ref=place, dst_ref=place, send_sem=o_send.at[h], recv_sem=o_recv.at[h],
            device_id=ynb, device_id_type=MESH,
        ).wait_recv()

        @pl.when(is_feeder)
        def _():
            feed_o(h, 1 - yi).start()

    def one_head(h, carry):
        def arrived(d, inner):
            for a in range(3):
                qkv_arrival(a, h, (ctx + d) % 8).wait_recv()
            return inner

        lax.fori_loop(1, 8, arrived, 0)
        for a in range(3):
            qkv_local(a, h).wait()
        for t in range(4):
            length = block * (t + 1)
            scores = lax.dot_general(
                qh[h, t * block : length, :], kh[h, :length, :],
                (((1,), (1,)), ((), ())), preferred_element_type=jnp.float32,
            )
            at_row = lax.broadcasted_iota(jnp.int32, (block, block), 0)
            at_col = lax.broadcasted_iota(jnp.int32, (block, block), 1)
            diagonal = jnp.where(at_row >= at_col, scores[:, t * block :], -1e30)
            if t > 0:
                scores = jnp.concatenate([scores[:, : t * block], diagonal], axis=1)
            else:
                scores = diagonal
            highest = jnp.max(scores, axis=-1, keepdims=True)
            expo = jnp.exp2((scores - highest) * factor)
            total = jnp.sum(expo, axis=-1, keepdims=True)
            result = jnp.dot(
                expo.astype(jnp.bfloat16), vh[h, :length, :], preferred_element_type=jnp.float32
            ) / total
            low, high = result[:rows], result[rows:]
            mine = jnp.where(yi == 0, low, high)
            theirs = jnp.where(yi == 0, high, low)
            op[yi, h, t * rows : (t + 1) * rows, :] = mine.astype(jnp.bfloat16)
            ostage[h, t * rows : (t + 1) * rows, :] = theirs.astype(jnp.bfloat16)
        o_copy(h).start()

        @pl.when(is_feeder)
        def _():
            feed_o(h, yi).start()

        @pl.when(h > 0)
        def _():
            other_half(h - 1)

        @pl.when(h == 1)
        def _():
            w_arrive(1, yi, xdp)
            forward(3, 1).start()

            @pl.when(is_hub)
            def _():
                forward(1, 0).start()

        @pl.when(jnp.logical_and(h == 2, is_hub))
        def _():
            w_arrive(2, yi, dp)
            forward(0, 2).start()
            forward(2, 2).start()
            w_arrive(0, yi, xdp)
            forward(3, 0).start()

        return carry

    lax.fori_loop(0, heads, one_head, 0)

    @pl.when(is_hub)
    def _():
        forward(1, 2).start()

    w_arrive(1, 1 - yi, dp)
    forward(5, 1).start()
    forward(4, 1).start()
    other_half(heads - 1)
    for part in range(2):
        keep_w(part).wait()

    def chain_copy(up, t, j, d):
        slot = t - 1 if up else t
        to = jnp.minimum(zi + 1, 3) if up else jnp.maximum(zi - 1, 0)
        return pltpu.make_async_remote_copy(
            src_ref=stages[j].at[slot, d],
            dst_ref=(uprs if up else dnrs)[j].at[slot, d],
            send_sem=(up_send if up else dn_send).at[slot, d * 2 + j],
            recv_sem=(up_recv if up else dn_recv).at[slot, d * 2 + j],
            device_id=(dp, to * 2 + yi),
            device_id_type=MESH,
        )

    def sends_here(up, t, hubs):
        sends = zi < t if up else zi > t
        if hubs:
            sends = jnp.logical_and(sends, zi >= 1 if up else zi <= 2)
        return sends

    def relay(up, t, j, d, allowed):
        hubs = j == 0
        slot = t - 1 if up else t
        there, stage, pbuf = (uprs if up else dnrs)[j], stages[j], pbufs[j]
        sends = jnp.logical_and(allowed, sends_here(up, t, hubs))
        first = (1 if hubs else 0) if up else (2 if hubs else 3)

        @pl.when(jnp.logical_and(sends, zi == first))
        def _():
            stage[slot, d] = pbuf[t].astype(jnp.bfloat16)
            chain_copy(up, t, j, d).start()

        @pl.when(jnp.logical_and(sends, zi != first))
        def _():
            chain_copy(up, t, j, d).wait_recv()
            stage[slot, d] = (pbuf[t] + there[slot, d].astype(jnp.float32)).astype(jnp.bfloat16)
            chain_copy(up, t, j, d).start()

    def relays(j, d):
        hubs = j == 0
        lower, upper = zi < 2, zi >= 2
        ups = (3, 2) if hubs else (3, 2, 1)
        downs = (0, 1) if hubs else (0, 1, 2)
        for t in ups:
            relay(True, t, j, d, lower)
        for t in downs:
            relay(False, t, j, d, upper)
        for t in ups:
            relay(True, t, j, d, upper)
        for t in downs:
            relay(False, t, j, d, lower)

    def owner(i):
        return ((xi + i // 2) % 2) * 2 + (core + i) % 2

    def wait_chain(up, slot, j, d):
        place = (uprs if up else dnrs)[j].at[slot, d]
        at = d * 2 + j
        pltpu.make_async_remote_copy(
            src_ref=place, dst_ref=place, send_sem=(up_send if up else dn_send).at[slot, at],
            recv_sem=(up_recv if up else dn_recv).at[slot, at], device_id=ynb, device_id_type=MESH,
        ).wait_recv()

    def finish(i, total):
        d = owner(i)
        for j in (1, 0):
            own = owns[j]

            @pl.when(zi > (1 if j == 0 else 0))
            def _():
                wait_chain(True, zi - 1, j, d)
                own[d] += uprs[j][zi - 1, d].astype(jnp.float32)

            @pl.when(zi < (2 if j == 0 else 3))
            def _():
                wait_chain(False, zi, j, d)
                own[d] += dnrs[j][zi, d].astype(jnp.float32)

            cols = pl.ds(pl.multiple_of(d * columns + starts[j], 128), chunks[j])
            res = res_ref[:, cols].astype(jnp.float32)
            mixed = deepnorm_alpha * res + own[d].astype(jnp.bfloat16).astype(jnp.float32)
            own[d] = mixed
            total = total + jnp.sum(mixed, axis=-1, keepdims=True)
        return total

    def heads_of(ref):
        return jnp.concatenate([ref[y, h] for y in range(2) for h in range(heads)], axis=1)

    def product(lhs, rhs):
        wide = rhs.shape[-1]
        return jnp.dot(
            lhs, rhs.reshape(2 * group, wide), preferred_element_type=jnp.float32
        ).reshape(4, rows, wide)

    def one_step(i, total):
        @pl.when(i < 4)
        def _():
            d = owner(i)

            @pl.when(i % 2 == 1)
            def _():
                for y in range(2):
                    w_arrive(1, y, d)

            pbuf_chain[...] = product(heads_of(op), wf_chain[:, d])
            relays(1, d)
            own_chain[d] = pbuf_chain[zi]

            @pl.when(i == 1)
            def _():
                w_arrive(1, 1 - yi, xdp)
                forward(6, 1).start()

        @pl.when(jnp.logical_and(i == 0, is_hub))
        def _():
            w_arrive(0, 1 - yi, dp)
            forward(5, 0).start()
            forward(4, 0).start()
            w_arrive(2, yi, xdp)
            forward(3, 2).start()

        @pl.when(jnp.logical_and(i == 1, is_hub))
        def _():
            w_arrive(2, 1 - yi, dp)
            forward(5, 2).start()
            forward(4, 2).start()
            for h in range(heads):
                for y in range(2):
                    place = op2.at[y, h]
                    pltpu.make_async_remote_copy(
                        src_ref=place, dst_ref=place, send_sem=o2_send.at[0, h],
                        recv_sem=o2_recv.at[y, h], device_id=ynb, device_id_type=MESH,
                    ).wait_recv()

        @pl.when(jnp.logical_and(i >= 1, is_hub))
        def _():
            d = owner(i - 1)

            @pl.when(i % 2 == 0)
            def _():
                for y in range(2):
                    w_arrive(0, y, d)
                    w_arrive(2, y, d)

            pbuf_hub[...] = product(heads_of(op), wf_hub[0, :, d])
            pbuf_hub[...] += product(heads_of(op2), wf_hub[1, :, d])
            relays(0, d)
            own_hub[d] = pbuf_hub[zi]

            @pl.when(i == 2)
            def _():
                for part in (0, 2):
                    w_arrive(part, 1 - yi, xdp)
                    forward(6, part).start()

        @pl.when(jnp.logical_and(i >= 1, is_feeder))
        def _():
            own_hub[owner(i - 1)] = jnp.zeros(own_hub.shape[1:], jnp.float32)

        return lax.cond(i > 2, lambda: finish(i - 3, total), lambda: total)

    total = lax.fori_loop(0, 5, one_step, jnp.zeros((rows, 1), jnp.float32))
    total = finish(2, total)
    total = finish(3, total)

    width = columns * 4
    mean = total / width
    squares = jnp.zeros((rows, 1), jnp.float32)
    for own in owns:
        for d in range(4):
            centered = own[d] - mean
            squares += jnp.sum(centered * centered, axis=-1, keepdims=True)
    inverse = lax.rsqrt(squares / width + norm_eps)
    for j, own in enumerate(owns):
        for d in range(4):
            low = d * columns + starts[j]
            cols = slice(low, low + chunks[j])
            normed = (own[d] - mean) * inverse * gain_ref[:, cols] + bias_ref[:, cols]
            out_ref[:, cols] = normed.astype(out_ref.dtype)

    def sent_qkv(h, carry):
        def sent(d, inner):
            for a in range(3):
                qkv_copy(a, h, (ctx + d) % 8).wait_send()
            return inner

        lax.fori_loop(1, 8, sent, 0)
        o_copy(h).wait_send()

        @pl.when(is_feeder)
        def _():
            feed_o(h, 0).wait_send()
            feed_o(h, 1).wait_send()

        return carry

    lax.fori_loop(0, heads, sent_qkv, 0)
    for number in routes:
        forward(number, 1).wait_send()

    @pl.when(is_feeder)
    def _():
        feed_w().wait_send()

    @pl.when(is_hub)
    def _():
        for number in routes:
            for part in (0, 2):
                forward(number, part).wait_send()

    def sent_chain(d, carry):
        for j in range(2):
            for up, targets in ((True, (3, 2, 1)), (False, (0, 1, 2))):
                for t in targets:
                    @pl.when(sends_here(up, t, j == 0))
                    def _():
                        chain_copy(up, t, j, d).wait_send()
        return carry

    lax.fori_loop(0, 4, sent_chain, 0)


def local_fused(queries, keys, values, residual_in, out_weight, norm_gain, norm_bias):
    rows, width = residual_in.shape
    group, columns = out_weight.shape
    hd = queries.shape[1] // HEADS
    heads = group // hd
    length = rows * 8
    hub_part = columns // 7 * 2
    chain_part = columns - hub_part
    bf16, f32 = jnp.bfloat16, jnp.float32
    dma = pltpu.SemaphoreType.DMA
    in_vmem = pl.BlockSpec(memory_space=pltpu.VMEM)
    in_any = pl.BlockSpec(memory_space=pl.ANY)
    return pl.pallas_call(
        fused_kernel,
        out_shape=jax.ShapeDtypeStruct((rows, width), bf16),
        in_specs=[in_any] * 4 + [in_vmem] * 3,
        out_specs=in_vmem,
        scratch_shapes=[
            pltpu.VMEM((heads, length, hd), bf16),
            pltpu.VMEM((heads, length, hd), bf16),
            pltpu.VMEM((heads, length, hd), bf16),
            pltpu.VMEM((2, 2, 4, group, hub_part), bf16),
            pltpu.VMEM((2, 4, group, chain_part), bf16),
            pltpu.VMEM((2, heads, length // 2, hd), bf16),
            pltpu.VMEM((2, heads, length // 2, hd), bf16),
            pltpu.VMEM((heads, length // 2, hd), bf16),
        ] + [
            pltpu.VMEM(shape + (rows, part), kind)
            for part in (hub_part, chain_part)
            for shape, kind in (((3, 4), bf16),) * 3 + (((4,), f32),) * 2
        ] + [
            dma((3, heads, 8)), dma((3, heads, 8)), dma((3, heads)),
            dma((8, 3)), dma((3, 2, 4)), dma((2,)),
            dma((heads,)), dma((heads,)), dma((2, heads)), dma((2, heads)),
            dma((3, 8)), dma((3, 8)), dma((3, 8)), dma((3, 8)),
        ],
        compiler_params=pltpu.CompilerParams(
            collective_id=0, has_side_effects=True, vmem_limit_bytes=60 * 1024 * 1024
        ),
    )(
        queries, keys, values, out_weight, residual_in,
        norm_gain.reshape(1, width), norm_bias.reshape(1, width),
    )


def solution(mesh):
    in_specs = (
        P(("dp", "ctx"), None),
        P(("dp", "ctx"), None),
        P(("dp", "ctx"), None),
        P(("dp", "ctx"), None),
        P("ctx", "dp"),
        P(),
        P(),
    )
    out_specs = P(("dp", "ctx"), None)
    fused = mesh.shape["dp"] == 4 and mesh.shape["ctx"] == 8
    local = local_fused if fused else local_general
    return jax.shard_map(local, mesh=mesh, in_specs=in_specs, out_specs=out_specs, check_vma=False)
```
